128 devices in a mesh: slot: 16 (over z_lo, x, core), param: 8 (over z_hi, y).
Axes of the slice: x: 4, y: 4, z: 4 (z_hi: 2, z_lo: 2; z = z_hi * 2 + z_lo), core: 2. Of those that a mesh axis runs over, the one named last changes fastest.
Arguments:
- history: float32 [256, 2048, 1024], P('slot', 'param'), may hold values from -6 to 6
- per_example: bfloat16 [64, 2048, 1024], P('slot', 'param')
- fresh: float32 [2048, 1024], P(('param', 'slot')), may hold values from -6 to 6
- moment1: float32 [2048, 1024], P(('param', 'slot')), may hold values from -4 to 4
- moment2: float32 [2048, 1024], P(('param', 'slot')), may hold values from 0.001 to 0.1
- master: float32 [2048, 1024], P(('param', 'slot')), may hold values from -6 to 6
- coef_table: float32 [64, 257], replicated, as said below
- table_index: int32 [1], replicated, may hold values from 0 to 63
- step_number: int32 [1], replicated, may hold values from 0 to 511
- cycle_slot: int32 [1], replicated, may hold values from 0 to 255
Outputs:
- new_noise: float32 [2048, 1024], P(('param', 'slot'))
- moment1_new: float32 [2048, 1024], P(('param', 'slot'))
- moment2_new: float32 [2048, 1024], P(('param', 'slot'))
- master_new: float32 [2048, 1024], P(('param', 'slot'))
- weights: bfloat16 [2048, 1024], P('param')
The draws below stay inside these ranges and needn't reach their ends.
Inputs may be any that keep to these rules, and one draw needn't show every extreme that they name: `coef_table`: column 0 lies in [1, 2].
All inputs are finite; a program needn't handle non-finite values.
Results may differ from the reference program's by a relative error of at most 0.008.
Values may be sent and summed in bfloat16 or wider, within the bound.
No kernel may reach another device: no remote copies, remote signals or barrier semaphores. Data moves between devices by JAX's collectives and lax.ppermute only.
A program may use at most 64 MiB of HBM per device.

```python
import math
import jax
import jax.numpy as jnp
from jax import lax

BAND = 256
LANES = 1024
TABLES = 64
ROWS_G = 256
PROWS = 2048
EXAMPLES = 64


def log_spread(key, shape, low, high):
    return jnp.exp(jax.random.uniform(key, shape, jnp.float32, math.log(low), math.log(high)))


def draw_per_example(key, part):
    key = jax.random.fold_in(key, 11)
    keys = jax.random.split(key, 5)
    blocks = PROWS // ROWS_G
    example_scale = log_spread(keys[0], (EXAMPLES, 1, 1), 0.02, 0.5)
    row_scale = log_spread(keys[1], (EXAMPLES, PROWS, 1), 0.5, 2.0)
    lane_scale = log_spread(keys[2], (EXAMPLES, 1, LANES), 0.5, 2.0)
    block_level = log_spread(keys[3], (EXAMPLES, blocks), 1.0, 10.0)
    base = jax.random.normal(keys[4], (EXAMPLES, PROWS, LANES), jnp.float32)
    level_rows = jnp.repeat(block_level, ROWS_G, axis=1)[:, :, None]
    return (example_scale * level_rows * row_scale * lane_scale * base).astype(jnp.bfloat16)


def draw_coef_table(key, part):
    key = jax.random.fold_in(key, 23)
    key_diag, key_rest = jax.random.split(key)
    diagonal = jax.random.uniform(key_diag, (TABLES, 1), jnp.float32, 1.0, 2.0)
    rest = 0.08 * jax.random.normal(key_rest, (TABLES, BAND), jnp.float32)
    return jnp.concatenate([diagonal, rest], axis=1)


def levels(own_key, dims, pieces, least, top_value):
    def one(position, shards_of):
        steps = jax.random.uniform(jax.random.fold_in(jax.random.fold_in(own_key, 6), position), (shards_of,), jnp.float32, least / len(pieces), top_value / len(pieces))
        return jnp.repeat(jnp.exp(steps), dims[position] // shards_of).reshape((-1,) + (1,) * (len(dims) - position - 1))

    gain = one(*pieces[0])
    for cut in pieces[1:]:
        gain = gain * one(*cut)
    return gain


def normal_values(stream_key, shape, spread, bound, shards=(), kind=jnp.bfloat16):
    array = jax.random.normal(stream_key, shape, jnp.float32) * spread
    if len(shards) > 0:
        array = levels(stream_key, shape, shards, -0.22, 0.18) * array
    return jnp.clip(array, min=-bound, max=bound).astype(kind)


def setup_inputs(seed: int = 0) -> dict:
    splits = jax.random.split(jax.random.key(seed), 11)
    return {
        "history": normal_values(splits[0], (BAND, PROWS, LANES), 1.0, 6.0, ((0, 16), (1, 8)), jnp.float32),
        "per_example": draw_per_example(jax.random.fold_in(splits[10], 71), 0),
        "fresh": normal_values(splits[2], (PROWS, LANES), 1.0, 6.0, ((0, 128),), jnp.float32),
        "moment1": normal_values(splits[3], (PROWS, LANES), 0.3, 4.0, ((0, 128),), jnp.float32),
        "moment2": jnp.clip(jnp.exp(math.log(0.1) - 4.6051702 * jax.random.uniform(splits[4], (PROWS, LANES), jnp.float32) ** levels(splits[4], (PROWS, LANES), ((0, 128),), -0.2, 0.2)), 0.001, 0.1),
        "master": normal_values(splits[5], (PROWS, LANES), 1.0, 6.0, ((0, 128),), jnp.float32),
        "coef_table": draw_coef_table(jax.random.fold_in(splits[10], 71), 0),
        "table_index": jax.random.randint(splits[7], (1,), 0, TABLES).astype(jnp.int32),
        "step_number": jax.random.randint(splits[8], (1,), 0, 2 * BAND).astype(jnp.int32),
        "cycle_slot": jax.random.randint(splits[9], (1,), 0, BAND).astype(jnp.int32),
    }


def reference(history, per_example, fresh, moment1, moment2, master, coef_table, table_index, step_number, cycle_slot):
    coefs = coef_table[table_index[0]]
    step = step_number[0]
    cycle = cycle_slot[0]
    slots = jnp.arange(BAND, dtype=jnp.int32)
    lag = ((cycle - slots - 1) % BAND + 1).astype(jnp.int32)
    slot_weight = jnp.where(lag <= step, coefs[lag], jnp.float32(0.0)).astype(jnp.float32)
    past = jnp.tensordot(slot_weight, history, axes=1, precision=lax.Precision.HIGHEST)
    new_noise = (fresh - past) / coefs[0]
    grads = per_example.astype(jnp.float32)
    sumsq = jnp.einsum('erl,erl->e', grads, grads, precision=lax.Precision.HIGHEST)
    rms = jnp.sqrt(sumsq / (PROWS * LANES))
    factor = 1.0 / jnp.maximum(rms, 1.0)
    clipped = jnp.einsum('e,erl->rl', factor, grads, precision=lax.Precision.HIGHEST)
    noisy = clipped + new_noise
    count = (step + 1).astype(jnp.float32)
    moment1_new = 0.9 * moment1 + 0.1 * noisy
    moment2_new = 0.999 * moment2 + 0.001 * noisy * noisy
    first_fix = 1.0 - jnp.power(jnp.float32(0.9), count)
    second_fix = 1.0 - jnp.power(jnp.float32(0.999), count)
    update = moment1_new / first_fix / (jnp.sqrt(moment2_new / second_fix) + 1e-08)
    master_new = master - 0.01 * update
    return (new_noise, moment1_new, moment2_new, master_new, master_new.astype(jnp.bfloat16))
```

```python
import jax
import jax.numpy as jnp
from jax import lax
from jax.experimental import pallas as pl
from jax.experimental.pallas import tpu as pltpu
from jax.sharding import PartitionSpec as P

MIB = 2**20
CORES = 2
VM = pl.BlockSpec(memory_space=pltpu.VMEM)
SM = pl.BlockSpec(memory_space=pltpu.SMEM)
HBM = pl.BlockSpec(memory_space=pl.ANY)


def params(mib):
    return pltpu.CompilerParams(vmem_limit_bytes=mib * MIB)


def core_index():
    return lax.rem(lax.axis_index("slot"), CORES)


def coef_row(coef_ref, index):
    row = lax.broadcasted_iota(jnp.int32, coef_ref.shape, 0)
    return jnp.sum(jnp.where(row == index, coef_ref[...], 0.0), axis=0, keepdims=True)


def square_kernel(grads_ref, out_ref, scratch):
    e = pl.program_id(0)
    total = jnp.zeros((8, 128), jnp.float32)
    for r in range(0, 256, 16):
        x = grads_ref[0, r : r + 16].astype(jnp.float32)
        x = x * x
        x = x[:8] + x[8:]
        for c in range(0, 1024, 128):
            total = total + x[:, c : c + 128]
    scratch[e] = jnp.broadcast_to(jnp.sum(total), (8, 128))

    @pl.when(e == 3)
    def _():
        rows = jnp.concatenate([scratch[k, 0:1] for k in range(4)] * 2, axis=0)
        for k in range(out_ref.shape[0]):
            out_ref[k] = rows


def squares(per_example):
    return pl.pallas_call(
        square_kernel,
        grid=(4,),
        in_specs=[pl.BlockSpec((1, 256, 1024), lambda e: (e, 0, 0))],
        out_specs=pl.BlockSpec((16, 8, 128), lambda e: (0, 0, 0)),
        out_shape=jax.ShapeDtypeStruct((16, 8, 128), jnp.float32),
        scratch_shapes=[pltpu.VMEM((4, 8, 128), jnp.float32)],
        compiler_params=params(8),
        cost_estimate=pl.CostEstimate(flops=2**30, bytes_accessed=32 * MIB, transcendentals=0),
        name="squares",
    )(per_example)


def past_kernel(table_ref, step_ref, cycle_ref, coef_ref, history_ref, keep_ref, send_ref, weight):
    slots = history_ref.shape[0]
    core = core_index()
    coefs = coef_row(coef_ref, table_ref[0])
    first = lax.axis_index("slot") * slots
    slot = first + lax.broadcasted_iota(jnp.int32, (slots, 1), 0)
    lag = ((cycle_ref[0] - slot - 1) & 255) + 1
    lane = lax.broadcasted_iota(jnp.int32, (slots, coefs.shape[1]), 1)
    picked = jnp.sum(jnp.where(lane == lag, coefs, 0.0), axis=1, keepdims=True)
    picked = jnp.where(lag <= step_ref[0], picked, 0.0)
    weight[...] = jnp.broadcast_to(picked, weight.shape)

    for part, out_ref in ((1 - core, send_ref), (core, keep_ref)):

        @pl.loop(0, 8)
        def _(b, part=part, out_ref=out_ref):
            for r in (0, 8):
                total = weight[0:1, :] * history_ref[0, b, part, r : r + 8, :]
                for s in range(1, slots):
                    total = total + weight[s : s + 1, :] * history_ref[s, b, part, r : r + 8, :]
                out_ref[b, r : r + 8, :] = total.astype(out_ref.dtype)


def past_parts(table_index, step_number, cycle_slot, coef_table, history):
    return pl.pallas_call(
        past_kernel,
        in_specs=[SM, SM, SM, VM, VM],
        out_specs=(VM, VM),
        out_shape=(
            jax.ShapeDtypeStruct((8, 16, 1024), jnp.float32),
            jax.ShapeDtypeStruct((8, 16, 1024), jnp.bfloat16),
        ),
        scratch_shapes=[pltpu.VMEM((16, 1024), jnp.float32)],
        compiler_params=params(24),
        cost_estimate=pl.CostEstimate(flops=8 * MIB, bytes_accessed=17 * MIB, transcendentals=0),
        name="past_parts",
    )(table_index, step_number, cycle_slot, coef_table, history)


def pack_kernel(sums_ref, own_ref, other_ref, keep_ref, got_ref, out_ref, factor):
    core = core_index()
    for side, part in ((0, core), (1, 1 - core)):
        total = sums_ref[0, part]
        for k in range(1, 8):
            total = total + sums_ref[k, part]
        rms = jnp.sqrt(total / (2048.0 * 1024.0))
        one = 1.0 / jnp.maximum(rms, 1.0)
        factor[side] = jnp.broadcast_to(one[:, 0:1], factor.shape[1:])

    @pl.loop(0, 8)
    def _(b):
        out_ref[b, 0] = (keep_ref[b] + got_ref[b].astype(jnp.float32)).astype(jnp.bfloat16)
        total = jnp.zeros((16, 1024), jnp.float32)
        for e in range(4):
            total = total + factor[0, e : e + 1, :] * own_ref[e, b, core].astype(jnp.float32)
            total = total + factor[1, e : e + 1, :] * other_ref[e, b, core].astype(jnp.float32)
        out_ref[b, 1] = total.astype(jnp.bfloat16)


def pack(sums, own, other, keep, got):
    return pl.pallas_call(
        pack_kernel,
        in_specs=[VM] * 5,
        out_specs=VM,
        out_shape=jax.ShapeDtypeStruct((8, 2, 16, 1024), jnp.bfloat16),
        scratch_shapes=[pltpu.VMEM((2, 8, 1024), jnp.float32)],
        compiler_params=params(12),
        cost_estimate=pl.CostEstimate(flops=4 * MIB, bytes_accessed=5 * MIB, transcendentals=0),
        name="pack",
    )(sums, own, other, keep, got)


def adam_kernel(
    table_ref, step_ref, coef_ref, parts_ref, fresh_ref, m1_ref, m2_ref, master_ref,
    noise_out, m1_out, m2_out, master_out, weights_out,
):
    past = parts_ref[0, 0].astype(jnp.float32)
    clipped = parts_ref[0, 1].astype(jnp.float32)
    for k in range(1, 8):
        past = past + parts_ref[k, 0].astype(jnp.float32)
        clipped = clipped + parts_ref[k, 1].astype(jnp.float32)
    first = coef_row(coef_ref, table_ref[0])[:, 0:1]
    new_noise = (fresh_ref[...] - past) / first
    noisy = clipped + new_noise
    count = jnp.full((1, 1), step_ref[0] + 1, jnp.int32).astype(jnp.float32)
    first_fix = 1.0 - jnp.power(jnp.float32(0.9), count)
    second_fix = 1.0 - jnp.power(jnp.float32(0.999), count)
    m1 = 0.9 * m1_ref[...] + 0.1 * noisy
    m2 = 0.999 * m2_ref[...] + 0.001 * noisy * noisy
    update = m1 / first_fix / (jnp.sqrt(m2 / second_fix) + 1e-08)
    master = master_ref[...] - 0.01 * update
    noise_out[...] = new_noise
    m1_out[...] = m1
    m2_out[...] = m2
    master_out[...] = master
    weights = master.astype(jnp.bfloat16)
    for k in range(8):
        weights_out[k] = weights


def adam(table_index, step_number, coef_table, parts, fresh, moment1, moment2, master):
    row = jax.ShapeDtypeStruct(fresh.shape, jnp.float32)
    return pl.pallas_call(
        adam_kernel,
        in_specs=[SM, SM] + [VM] * 6,
        out_specs=(VM,) * 5,
        out_shape=(row, row, row, row, jax.ShapeDtypeStruct((8, 16, 1024), jnp.bfloat16)),
        compiler_params=params(8),
        cost_estimate=pl.CostEstimate(flops=MIB, bytes_accessed=2 * MIB, transcendentals=0),
        name="adam",
    )(table_index, step_number, coef_table, parts, fresh, moment1, moment2, master)


def weave_kernel(own_ref, other_ref, out_ref, sems):
    core = core_index()
    a = pltpu.make_async_copy(own_ref, out_ref.at[:, core], sems.at[0])
    b = pltpu.make_async_copy(other_ref, out_ref.at[:, 1 - core], sems.at[1])
    a.start()
    b.start()
    a.wait()
    b.wait()


def weave(own, other):
    return pl.pallas_call(
        weave_kernel,
        in_specs=[HBM, HBM],
        out_specs=HBM,
        out_shape=jax.ShapeDtypeStruct((8, 2, 16, 1024), jnp.bfloat16),
        scratch_shapes=[pltpu.SemaphoreType.DMA((2,))],
        compiler_params=params(4),
        name="weave",
    )(own, other)


def shards(
    history,
    per_example,
    fresh,
    moment1,
    moment2,
    master,
    coef_table,
    table_index,
    step_number,
    cycle_slot,
):
    swap = [(i, i ^ 1) for i in range(16)]
    one_core = [[2 * k + c for k in range(8)] for c in range(2)]
    chips = [[16 * p + 2 * k + c for p in range(8) for c in range(2)] for k in range(8)]
    other_example = lax.ppermute(per_example, "slot", swap)
    sums = lax.all_to_all(
        squares(per_example), ("param", "slot"), 0, 0, tiled=True, axis_index_groups=chips
    )
    keep, send = past_parts(
        table_index, step_number, cycle_slot, coef_table, history.reshape(16, 8, 2, 16, 1024)
    )
    got = lax.ppermute(send, "slot", swap)
    packed = pack(
        sums.reshape(8, 2, 8, 128),
        per_example.reshape(4, 8, 2, 16, 1024),
        other_example.reshape(4, 8, 2, 16, 1024),
        keep,
        got,
    )
    parts = lax.all_to_all(packed, "slot", 0, 0, tiled=True, axis_index_groups=one_core)
    new_noise, m1, m2, master_new, weights = adam(
        table_index, step_number, coef_table, parts, fresh, moment1, moment2, master
    )
    gathered = lax.all_to_all(weights, "slot", 0, 0, tiled=True, axis_index_groups=one_core)
    gathered = weave(gathered, lax.ppermute(gathered, "slot", swap))
    return (new_noise, m1, m2, master_new, gathered.reshape(256, 1024))


def solution(mesh):
    placed = (
        P("slot", "param", None),
        P("slot", "param", None),
        P(("param", "slot"), None),
        P(("param", "slot"), None),
        P(("param", "slot"), None),
        P(("param", "slot"), None),
        P(),
        P(),
        P(),
        P(),
    )
    return jax.shard_map(
        shards,
        mesh=mesh,
        in_specs=placed,
        out_specs=(
            P(("param", "slot"), None),
            P(("param", "slot"), None),
            P(("param", "slot"), None),
            P(("param", "slot"), None),
            P("param", None),
        ),
        check_vma=False,
    )
```

```python
import functools

import jax
import jax.numpy as jnp
from jax import lax
from jax.experimental import pallas as pl
from jax.experimental.pallas import tpu as pltpu
from jax.sharding import PartitionSpec as P

MIB = 2**20
CORES = 2
VM = pl.BlockSpec(memory_space=pltpu.VMEM)
HBM = pl.BlockSpec(memory_space=pl.ANY)


def params(mib):
    return pltpu.CompilerParams(vmem_limit_bytes=mib * MIB)


def core_index():
    return lax.rem(lax.axis_index("slot"), CORES)


def coef_row(coef_ref, index):
    row = lax.broadcasted_iota(jnp.int32, coef_ref.shape, 0)
    return jnp.sum(jnp.where(row == index, coef_ref[...], 0.0), axis=0, keepdims=True)


def square_kernel(grads_ref, out_ref):
    rows = []
    for e in range(4):
        total = [jnp.zeros((16, 128), jnp.float32) for _ in range(4)]
        for r in range(0, 256, 16):
            for c in range(0, 1024, 128):
                x = grads_ref[e, r : r + 16, c : c + 128].astype(jnp.float32)
                total[(c // 128) % 4] = total[(c // 128) % 4] + x * x
        total = (total[0] + total[1]) + (total[2] + total[3])
        rows.append(jnp.broadcast_to(jnp.sum(total), (1, 128)))
    rows = jnp.concatenate(rows * 2, axis=0)
    core = lax.broadcasted_iota(jnp.int32, rows.shape, 0) // 4
    out_ref[...] = jnp.where(core == core_index(), rows, 0.0)


def squares(per_example):
    return pl.pallas_call(
        square_kernel,
        in_specs=[VM],
        out_specs=VM,
        out_shape=jax.ShapeDtypeStruct((8, 128), jnp.float32),
        compiler_params=params(8),
        cost_estimate=pl.CostEstimate(flops=2**30, bytes_accessed=64 * MIB, transcendentals=0),
        name="squares",
    )(per_example)


def past_kernel(side, table_ref, step_ref, cycle_ref, coef_ref, history_ref, _, out_ref, weight):
    slots = history_ref.shape[0]
    part = core_index()
    if side:
        part = 1 - part
    coefs = coef_row(coef_ref, table_ref[...])
    first = lax.axis_index("slot") * slots
    slot = first + lax.broadcasted_iota(jnp.int32, (slots, 1), 0)
    lag = ((cycle_ref[...] - slot - 1) & 255) + 1
    lane = lax.broadcasted_iota(jnp.int32, (slots, coefs.shape[1]), 1)
    picked = jnp.sum(jnp.where(lane == lag, coefs, 0.0), axis=1, keepdims=True)
    picked = jnp.where(lag <= step_ref[...], picked, 0.0)
    weight[...] = jnp.broadcast_to(picked, weight.shape)

    @pl.loop(0, 8)
    def _(b):
        for r in (0, 8):
            total = weight[0:1, :] * history_ref[0, b, part, r : r + 8, :]
            for s in range(1, slots):
                total = total + weight[s : s + 1, :] * history_ref[s, b, part, r : r + 8, :]
            out_ref[b, r : r + 8, :] = total.astype(out_ref.dtype)


def past_part(side, dtype, table_index, step_number, cycle_slot, coef_table, history, after):
    return pl.pallas_call(
        functools.partial(past_kernel, side),
        in_specs=[VM] * 5 + [HBM],
        out_specs=VM,
        out_shape=jax.ShapeDtypeStruct((8, 16, 1024), dtype),
        scratch_shapes=[pltpu.VMEM((16, 1024), jnp.float32)],
        compiler_params=params(4),
        cost_estimate=pl.CostEstimate(flops=4 * MIB, bytes_accessed=8 * MIB, transcendentals=0),
        name="past_part",
    )(table_index, step_number, cycle_slot, coef_table, history, after)


def pack_kernel(sums_ref, last_ref, own_ref, other_ref, keep_ref, got_ref, out_ref, factor):
    core = core_index()
    rms = jnp.sqrt((sums_ref[...] + last_ref[...]) / (2048.0 * 1024.0))
    one = 1.0 / jnp.maximum(rms, 1.0)
    factor[0] = jnp.broadcast_to(jnp.where(core == 0, one[0:4, 0:1], one[4:8, 0:1]), factor.shape[1:])
    factor[1] = jnp.broadcast_to(jnp.where(core == 0, one[4:8, 0:1], one[0:4, 0:1]), factor.shape[1:])

    @pl.loop(0, 8)
    def _(b):
        out_ref[b, 0] = (keep_ref[b] + got_ref[b].astype(jnp.float32)).astype(jnp.bfloat16)
        total = jnp.zeros((16, 1024), jnp.float32)
        for e in range(4):
            total = total + factor[0, e : e + 1, :] * own_ref[e, b, core].astype(jnp.float32)
            total = total + factor[1, e : e + 1, :] * other_ref[e, b, core].astype(jnp.float32)
        out_ref[b, 1] = total.astype(jnp.bfloat16)


def pack(sums, last, own, other, keep, got):
    return pl.pallas_call(
        pack_kernel,
        in_specs=[VM] * 6,
        out_specs=VM,
        out_shape=jax.ShapeDtypeStruct((8, 2, 16, 1024), jnp.bfloat16),
        scratch_shapes=[pltpu.VMEM((2, 4, 1024), jnp.float32)],
        compiler_params=params(12),
        cost_estimate=pl.CostEstimate(flops=4 * MIB, bytes_accessed=5 * MIB, transcendentals=0),
        name="pack",
    )(sums, last, own, other, keep, got)


def adam_kernel(
    table_ref, step_ref, coef_ref, parts_ref, fresh_ref, m1_ref, m2_ref, master_ref,
    noise_out, m1_out, m2_out, master_out, weights_out,
):
    past = parts_ref[0, 0].astype(jnp.float32)
    clipped = parts_ref[0, 1].astype(jnp.float32)
    for k in range(1, 8):
        past = past + parts_ref[k, 0].astype(jnp.float32)
        clipped = clipped + parts_ref[k, 1].astype(jnp.float32)
    first = coef_row(coef_ref, table_ref[...])[:, 0:1]
    new_noise = (fresh_ref[...] - past) / first
    noisy = clipped + new_noise
    count = (step_ref[...] + 1).astype(jnp.float32)
    first_fix = 1.0 - jnp.power(jnp.float32(0.9), count)
    second_fix = 1.0 - jnp.power(jnp.float32(0.999), count)
    m1 = 0.9 * m1_ref[...] + 0.1 * noisy
    m2 = 0.999 * m2_ref[...] + 0.001 * noisy * noisy
    update = m1 / first_fix / (jnp.sqrt(m2 / second_fix) + 1e-08)
    master = master_ref[...] - 0.01 * update
    noise_out[...] = new_noise
    m1_out[...] = m1
    m2_out[...] = m2
    master_out[...] = master
    weights = master.astype(jnp.bfloat16)
    for k in range(8):
        weights_out[k] = weights


def adam(table_index, step_number, coef_table, parts, fresh, moment1, moment2, master):
    row = jax.ShapeDtypeStruct(fresh.shape, jnp.float32)
    return pl.pallas_call(
        adam_kernel,
        in_specs=[VM] * 8,
        out_specs=(VM,) * 5,
        out_shape=(row, row, row, row, jax.ShapeDtypeStruct((8, 16, 1024), jnp.bfloat16)),
        compiler_params=params(8),
        cost_estimate=pl.CostEstimate(flops=MIB, bytes_accessed=2 * MIB, transcendentals=0),
        name="adam",
    )(table_index, step_number, coef_table, parts, fresh, moment1, moment2, master)


def weave_kernel(own_ref, other_ref, out_ref, sems):
    core = core_index()
    a = pltpu.make_async_copy(own_ref, out_ref.at[:, core], sems.at[0])
    b = pltpu.make_async_copy(other_ref, out_ref.at[:, 1 - core], sems.at[1])
    a.start()
    b.start()
    a.wait()
    b.wait()


def weave(own, other):
    return pl.pallas_call(
        weave_kernel,
        in_specs=[HBM, HBM],
        out_specs=HBM,
        out_shape=jax.ShapeDtypeStruct((8, 2, 16, 1024), jnp.bfloat16),
        scratch_shapes=[pltpu.SemaphoreType.DMA((2,))],
        compiler_params=params(4),
        name="weave",
    )(own, other)


def shards(
    history,
    per_example,
    fresh,
    moment1,
    moment2,
    master,
    coef_table,
    table_index,
    step_number,
    cycle_slot,
):
    table_index, step_number, cycle_slot = (
        x.reshape(1, 1) for x in (table_index, step_number, cycle_slot)
    )
    swap = [(i, i ^ 1) for i in range(16)]
    one_core = [[2 * k + c for k in range(8)] for c in range(2)]
    near = [(i, i ^ 1) for i in range(8)]
    far = [(i, i ^ 3) for i in range(8)]
    across = [(i, i ^ 4) for i in range(8)]
    sums = squares(per_example)
    sums = sums + lax.ppermute(sums, "slot", swap)
    _, early = lax.optimization_barrier((sums, per_example))
    other_example = lax.ppermute(early, "slot", swap)
    sums = sums + lax.ppermute(sums, "param", near)
    sums = sums + lax.ppermute(sums, "param", far)
    last = lax.ppermute(sums, "param", across)
    blocks = history.reshape(16, 8, 2, 16, 1024)
    send = past_part(
        1, jnp.bfloat16, table_index, step_number, cycle_slot, coef_table, blocks, sums
    )
    got = lax.ppermute(send, "slot", swap)
    keep = past_part(
        0, jnp.float32, table_index, step_number, cycle_slot, coef_table, blocks, send
    )
    packed = pack(
        sums,
        last,
        per_example.reshape(4, 8, 2, 16, 1024),
        other_example.reshape(4, 8, 2, 16, 1024),
        keep,
        got,
    )
    parts = lax.all_to_all(packed, "slot", 0, 0, tiled=True, axis_index_groups=one_core)
    new_noise, m1, m2, master_new, weights = adam(
        table_index, step_number, coef_table, parts, fresh, moment1, moment2, master
    )
    gathered = lax.all_to_all(weights, "slot", 0, 0, tiled=True, axis_index_groups=one_core)
    gathered = weave(gathered, lax.ppermute(gathered, "slot", swap))
    return (new_noise, m1, m2, master_new, gathered.reshape(256, 1024))


def solution(mesh):
    placed = (
        P("slot", "param", None),
        P("slot", "param", None),
        P(("param", "slot"), None),
        P(("param", "slot"), None),
        P(("param", "slot"), None),
        P(("param", "slot"), None),
        P(),
        P(),
        P(),
        P(),
    )
    return jax.shard_map(
        shards,
        mesh=mesh,
        in_specs=placed,
        out_specs=(
            P(("param", "slot"), None),
            P(("param", "slot"), None),
            P(("param", "slot"), None),
            P(("param", "slot"), None),
            P("param", None),
        ),
        check_vma=False,
    )
```

```python
import functools

import jax
import jax.numpy as jnp
from jax import lax
from jax.experimental import pallas as pl
from jax.experimental.pallas import tpu as pltpu
from jax.sharding import PartitionSpec as P

MIB = 2**20
CORES = 2
SM = pl.BlockSpec(memory_space=pltpu.SMEM)
VM = pl.BlockSpec(memory_space=pltpu.VMEM)
HBM = pl.BlockSpec(memory_space=pl.ANY)


def params(mib):
    return pltpu.CompilerParams(vmem_limit_bytes=mib * MIB)


def core_index():
    return lax.rem(lax.axis_index("slot"), CORES)


def coef_row(coef_ref, index):
    row = lax.broadcasted_iota(jnp.int32, coef_ref.shape, 0)
    return jnp.sum(jnp.where(row == index, coef_ref[...], 0.0), axis=0, keepdims=True)


def square_kernel(grads_ref, out_ref):
    rows = []
    for e in range(4):
        total = [jnp.zeros((16, 128), jnp.float32) for _ in range(4)]
        for r in range(16):
            for c in range(0, 1024, 128):
                x = grads_ref[e, r // 2, r % 2, :, c : c + 128].astype(jnp.float32)
                total[(c // 128) % 4] = total[(c // 128) % 4] + x * x
        total = (total[0] + total[1]) + (total[2] + total[3])
        rows.append(jnp.broadcast_to(jnp.sum(total), (1, 128)))
    rows = jnp.concatenate(rows * 2, axis=0)
    core = lax.broadcasted_iota(jnp.int32, rows.shape, 0) // 4
    out_ref[...] = jnp.where(core == core_index(), rows, 0.0)


def squares(per_example):
    return pl.pallas_call(
        square_kernel,
        in_specs=[VM],
        out_specs=VM,
        out_shape=jax.ShapeDtypeStruct((8, 128), jnp.float32),
        compiler_params=params(8),
        cost_estimate=pl.CostEstimate(flops=2**37, bytes_accessed=2 * MIB, transcendentals=0),
        name="squares",
    )(per_example)


def past_kernel(table_ref, step_ref, cycle_ref, coef_ref, history_ref, _, keep_ref, send_ref, weight):
    slots = history_ref.shape[0]
    core = core_index()
    coefs = coef_row(coef_ref, table_ref[0])
    first = lax.axis_index("slot") * slots
    slot = first + lax.broadcasted_iota(jnp.int32, (slots, 1), 0)
    lag = ((cycle_ref[0] - slot - 1) & 255) + 1
    lane = lax.broadcasted_iota(jnp.int32, (slots, coefs.shape[1]), 1)
    picked = jnp.sum(jnp.where(lane == lag, coefs, 0.0), axis=1, keepdims=True)
    picked = jnp.where(lag <= step_ref[0], picked, 0.0)
    weight[...] = jnp.broadcast_to(picked, weight.shape)

    for part, out_ref in ((1 - core, send_ref), (core, keep_ref)):

        @pl.loop(0, 8)
        def _(b, part=part, out_ref=out_ref):
            for r in (0, 8):
                total = weight[0:1, :] * history_ref[0, b, part, r : r + 8, :]
                for s in range(1, slots):
                    total = total + weight[s : s + 1, :] * history_ref[s, b, part, r : r + 8, :]
                out_ref[b, r : r + 8, :] = total.astype(out_ref.dtype)


def past_parts(table_index, step_number, cycle_slot, coef_table, history, after):
    return pl.pallas_call(
        past_kernel,
        in_specs=[SM] * 3 + [VM] * 2 + [HBM],
        out_specs=(VM, VM),
        out_shape=(
            jax.ShapeDtypeStruct((8, 16, 1024), jnp.float32),
            jax.ShapeDtypeStruct((8, 16, 1024), jnp.bfloat16),
        ),
        scratch_shapes=[pltpu.VMEM((16, 1024), jnp.float32)],
        compiler_params=params(4),
        cost_estimate=pl.CostEstimate(flops=1, bytes_accessed=1, transcendentals=0),
        name="past_parts",
    )(table_index, step_number, cycle_slot, coef_table, history, after)


def add_kernel(a_ref, b_ref, out_ref):
    out_ref[...] = a_ref[...] + b_ref[...]


def add(a, b):
    return pl.pallas_call(
        add_kernel,
        in_specs=[VM, VM],
        out_specs=VM,
        out_shape=jax.ShapeDtypeStruct(a.shape, a.dtype),
        compiler_params=params(4),
        cost_estimate=pl.CostEstimate(flops=2**34, bytes_accessed=12288, transcendentals=0),
        name="add",
    )(a, b)


def pack_kernel(sums_ref, last_ref, own_ref, other_ref, keep_ref, got_ref, out_ref, factor):
    core = core_index()
    rms = jnp.sqrt((sums_ref[...] + last_ref[...]) / (2048.0 * 1024.0))
    one = 1.0 / jnp.maximum(rms, 1.0)
    factor[0] = jnp.broadcast_to(jnp.where(core == 0, one[0:4, 0:1], one[4:8, 0:1]), factor.shape[1:])
    factor[1] = jnp.broadcast_to(jnp.where(core == 0, one[4:8, 0:1], one[0:4, 0:1]), factor.shape[1:])

    @pl.loop(0, 8)
    def _(b):
        out_ref[b, 0] = (keep_ref[b] + got_ref[b].astype(jnp.float32)).astype(jnp.bfloat16)
        total = jnp.zeros((16, 1024), jnp.float32)
        for e in range(4):
            total = total + factor[0, e : e + 1, :] * own_ref[e, b, core].astype(jnp.float32)
            total = total + factor[1, e : e + 1, :] * other_ref[e, b, core].astype(jnp.float32)
        out_ref[b, 1] = total.astype(jnp.bfloat16)


def pack(sums, last, own, other, keep, got):
    return pl.pallas_call(
        pack_kernel,
        in_specs=[VM] * 6,
        out_specs=VM,
        out_shape=jax.ShapeDtypeStruct((8, 2, 16, 1024), jnp.bfloat16),
        scratch_shapes=[pltpu.VMEM((2, 4, 1024), jnp.float32)],
        compiler_params=params(12),
        cost_estimate=pl.CostEstimate(flops=4 * MIB, bytes_accessed=5 * MIB, transcendentals=0),
        name="pack",
    )(sums, last, own, other, keep, got)


def adam_kernel(
    table_ref, step_ref, coef_ref, parts_ref, fresh_ref, m1_ref, m2_ref, master_ref,
    noise_out, m1_out, m2_out, master_out, weights_out,
):
    past = parts_ref[0, 0].astype(jnp.float32)
    clipped = parts_ref[0, 1].astype(jnp.float32)
    for k in range(1, 8):
        past = past + parts_ref[k, 0].astype(jnp.float32)
        clipped = clipped + parts_ref[k, 1].astype(jnp.float32)
    first = coef_row(coef_ref, table_ref[0])[:, 0:1]
    new_noise = (fresh_ref[...] - past) / first
    noisy = clipped + new_noise
    count = jnp.full((1, 1), step_ref[0] + 1, jnp.int32).astype(jnp.float32)
    first_fix = 1.0 - jnp.power(jnp.float32(0.9), count)
    second_fix = 1.0 - jnp.power(jnp.float32(0.999), count)
    m1 = 0.9 * m1_ref[...] + 0.1 * noisy
    m2 = 0.999 * m2_ref[...] + 0.001 * noisy * noisy
    update = m1 / first_fix / (jnp.sqrt(m2 / second_fix) + 1e-08)
    master = master_ref[...] - 0.01 * update
    noise_out[...] = new_noise
    m1_out[...] = m1
    m2_out[...] = m2
    master_out[...] = master
    weights = master.astype(jnp.bfloat16)
    for k in range(8):
        weights_out[k] = weights


def adam(table_index, step_number, coef_table, parts, fresh, moment1, moment2, master):
    row = jax.ShapeDtypeStruct(fresh.shape, jnp.float32)
    return pl.pallas_call(
        adam_kernel,
        in_specs=[SM] * 2 + [VM] * 6,
        out_specs=(VM,) * 5,
        out_shape=(row, row, row, row, jax.ShapeDtypeStruct((8, 16, 1024), jnp.bfloat16)),
        compiler_params=params(8),
        cost_estimate=pl.CostEstimate(flops=MIB, bytes_accessed=2 * MIB, transcendentals=0),
        name="adam",
    )(table_index, step_number, coef_table, parts, fresh, moment1, moment2, master)


def weave_kernel(own_ref, other_ref, out_ref, sems):
    core = core_index()
    a = pltpu.make_async_copy(own_ref, out_ref.at[:, core], sems.at[0])
    b = pltpu.make_async_copy(other_ref, out_ref.at[:, 1 - core], sems.at[1])
    a.start()
    b.start()
    a.wait()
    b.wait()


def weave(own, other):
    return pl.pallas_call(
        weave_kernel,
        in_specs=[HBM, HBM],
        out_specs=HBM,
        out_shape=jax.ShapeDtypeStruct((8, 2, 16, 1024), jnp.bfloat16),
        scratch_shapes=[pltpu.SemaphoreType.DMA((2,))],
        compiler_params=params(4),
        name="weave",
    )(own, other)


def shards(
    history,
    per_example,
    fresh,
    moment1,
    moment2,
    master,
    coef_table,
    table_index,
    step_number,
    cycle_slot,
):
    swap = [(i, i ^ 1) for i in range(16)]
    one_core = [[2 * k + c for k in range(8)] for c in range(2)]
    near = [(i, i ^ 1) for i in range(8)]
    far = [(i, i ^ 3) for i in range(8)]
    across = [(i, i ^ 4) for i in range(8)]
    examples = per_example.reshape(4, 8, 2, 16, 1024)
    sums = squares(examples)
    sums = sums + lax.ppermute(sums, "slot", swap)
    _, early = lax.optimization_barrier((sums, examples))
    other = lax.ppermute(early, "slot", swap)
    keep, send = past_parts(
        table_index, step_number, cycle_slot, coef_table, history.reshape(16, 8, 2, 16, 1024), sums
    )
    got = lax.ppermute(send, "slot", swap)
    sums = sums + lax.ppermute(sums, "param", across)
    sums, keep = lax.optimization_barrier((sums, keep))
    sums = add(sums, lax.ppermute(sums, "param", near))
    last = lax.ppermute(sums, "param", far)
    packed = pack(sums, last, examples, other, keep, got)
    parts = lax.all_to_all(packed, "slot", 0, 0, tiled=True, axis_index_groups=one_core)
    new_noise, m1, m2, master_new, weights = adam(
        table_index, step_number, coef_table, parts, fresh, moment1, moment2, master
    )
    gathered = lax.all_to_all(weights, "slot", 0, 0, tiled=True, axis_index_groups=one_core)
    gathered = weave(gathered, lax.ppermute(gathered, "slot", swap))
    return (new_noise, m1, m2, master_new, gathered.reshape(256, 1024))


def solution(mesh):
    placed = (
        P("slot", "param", None),
        P("slot", "param", None),
        P(("param", "slot"), None),
        P(("param", "slot"), None),
        P(("param", "slot"), None),
        P(("param", "slot"), None),
        P(),
        P(),
        P(),
        P(),
    )
    return jax.shard_map(
        shards,
        mesh=mesh,
        in_specs=placed,
        out_specs=(
            P(("param", "slot"), None),
            P(("param", "slot"), None),
            P(("param", "slot"), None),
            P(("param", "slot"), None),
            P("param", None),
        ),
        check_vma=False,
    )
```

```python
import functools

import jax
import jax.numpy as jnp
from jax import lax
from jax.experimental import pallas as pl
from jax.experimental.pallas import tpu as pltpu
from jax.sharding import PartitionSpec as P

MIB = 2**20
CORES = 2
SM = pl.BlockSpec(memory_space=pltpu.SMEM)
VM = pl.BlockSpec(memory_space=pltpu.VMEM)
HBM = pl.BlockSpec(memory_space=pl.ANY)


def params(mib):
    return pltpu.CompilerParams(vmem_limit_bytes=mib * MIB)


def core_index():
    return lax.rem(lax.axis_index("slot"), CORES)


def coef_row(coef_ref, index):
    row = lax.broadcasted_iota(jnp.int32, coef_ref.shape, 0)
    return jnp.sum(jnp.where(row == index, coef_ref[...], 0.0), axis=0, keepdims=True)


def square_kernel(grads_ref, out_ref, grads, sems):
    n = grads.shape[0]
    copies = [pltpu.make_async_copy(grads_ref.at[e], grads.at[e], sems.at[e]) for e in range(n)]
    for copy in copies:
        copy.start()
    for e in range(n):
        copies[e].wait()
        total = [jnp.zeros((16, 128), jnp.float32) for _ in range(4)]
        for r in range(16):
            for c in range(0, 1024, 128):
                x = grads[e, r // 2, r % 2, :, c : c + 128].astype(jnp.float32)
                total[(c // 128) % 4] = total[(c // 128) % 4] + x * x
        total = (total[0] + total[1]) + (total[2] + total[3])
        out_ref[e] = total[:8] + total[8:]


def squares(per_example):
    return pl.pallas_call(
        square_kernel,
        in_specs=[HBM],
        out_specs=VM,
        out_shape=jax.ShapeDtypeStruct((4, 8, 128), jnp.float32),
        scratch_shapes=[
            pltpu.VMEM(per_example.shape, per_example.dtype),
            pltpu.SemaphoreType.DMA((per_example.shape[0],)),
        ],
        compiler_params=params(8),
        cost_estimate=pl.CostEstimate(flops=1, bytes_accessed=2 * MIB, transcendentals=0),
        name="squares",
    )(pltpu.with_memory_space_constraint(per_example, pltpu.HBM))


def place_kernel(squares_ref, out_ref):
    rows = jnp.sum(squares_ref[...], axis=1)
    rows = jnp.broadcast_to(jnp.sum(rows, axis=1, keepdims=True), rows.shape)
    rows = jnp.concatenate([rows, rows], axis=0)
    core = lax.broadcasted_iota(jnp.int32, rows.shape, 0) // 4
    out_ref[...] = jnp.where(core == core_index(), rows, 0.0)


def place(sums):
    return pl.pallas_call(
        place_kernel,
        in_specs=[VM],
        out_specs=VM,
        out_shape=jax.ShapeDtypeStruct((8, 128), jnp.float32),
        compiler_params=params(4),
        cost_estimate=pl.CostEstimate(flops=2**37, bytes_accessed=2**14, transcendentals=0),
        name="place",
    )(sums)


def weights_kernel(table_ref, step_ref, cycle_ref, coef_ref, weight_ref, scalars_ref):
    slots = weight_ref.shape[0]
    coefs = coef_row(coef_ref, table_ref[0])
    first = lax.axis_index("slot") * slots
    slot = first + lax.broadcasted_iota(jnp.int32, (slots, 1), 0)
    lag = ((cycle_ref[0] - slot - 1) & 255) + 1
    lane = lax.broadcasted_iota(jnp.int32, (slots, coefs.shape[1]), 1)
    picked = jnp.sum(jnp.where(lane == lag, coefs, 0.0), axis=1, keepdims=True)
    picked = jnp.where(lag <= step_ref[0], picked, 0.0)
    weight_ref[...] = jnp.broadcast_to(picked[:, :, None], weight_ref.shape)
    row = lax.broadcasted_iota(jnp.int32, scalars_ref.shape, 0)
    count = jnp.full((1, 1), step_ref[0] + 1, jnp.int32).astype(jnp.float32)
    scalars_ref[...] = jnp.where(row == 0, coefs[:, 0:1], count)


def slot_weights(table_index, step_number, cycle_slot, coef_table):
    return pl.pallas_call(
        weights_kernel,
        in_specs=[SM] * 3 + [VM],
        out_specs=(VM, VM),
        out_shape=(
            jax.ShapeDtypeStruct((16, 8, 128), jnp.float32),
            jax.ShapeDtypeStruct((8, 128), jnp.float32),
        ),
        compiler_params=params(4),
        cost_estimate=pl.CostEstimate(flops=1, bytes_accessed=1, transcendentals=0),
        name="slot_weights",
    )(table_index, step_number, cycle_slot, coef_table)


def past_kernel(weight_ref, history_ref, _, keep_ref, send_ref):
    slots = history_ref.shape[0]
    core = core_index()
    for part, out_ref in ((1 - core, send_ref), (core, keep_ref)):

        @pl.loop(0, 8)
        def _(b, part=part, out_ref=out_ref):
            scale = [weight_ref[s] for s in range(slots)]
            for r in (0, 8):
                for c in range(0, 1024, 128):
                    total = scale[0] * history_ref[0, b, part, r : r + 8, c : c + 128]
                    for s in range(1, slots):
                        total = total + scale[s] * history_ref[s, b, part, r : r + 8, c : c + 128]
                    out_ref[b, r : r + 8, c : c + 128] = total.astype(out_ref.dtype)


def past_parts(weight, history, after):
    return pl.pallas_call(
        past_kernel,
        in_specs=[VM, VM, HBM],
        out_specs=(VM, VM),
        out_shape=(
            jax.ShapeDtypeStruct((8, 16, 1024), jnp.float32),
            jax.ShapeDtypeStruct((8, 16, 1024), jnp.bfloat16),
        ),
        compiler_params=params(4),
        cost_estimate=pl.CostEstimate(flops=1, bytes_accessed=1, transcendentals=0),
        name="past_parts",
    )(weight, history, after)


def add_kernel(a_ref, b_ref, out_ref):
    out_ref[...] = a_ref[...] + b_ref[...]


def add(a, b):
    return pl.pallas_call(
        add_kernel,
        in_specs=[VM, VM],
        out_specs=VM,
        out_shape=jax.ShapeDtypeStruct(a.shape, a.dtype),
        compiler_params=params(4),
        cost_estimate=pl.CostEstimate(flops=2**34, bytes_accessed=12288, transcendentals=0),
        name="add",
    )(a, b)


def pack_kernel(sums_ref, last_ref, own_ref, other_ref, keep_ref, got_ref, out_ref, factor):
    core = core_index()
    rms = jnp.sqrt((sums_ref[...] + last_ref[...]) / (2048.0 * 1024.0))
    one = 1.0 / jnp.maximum(rms, 1.0)
    factor[0] = jnp.broadcast_to(jnp.where(core == 0, one[0:4, 0:1], one[4:8, 0:1]), factor.shape[1:])
    factor[1] = jnp.broadcast_to(jnp.where(core == 0, one[4:8, 0:1], one[0:4, 0:1]), factor.shape[1:])

    @pl.loop(0, 8)
    def _(b):
        out_ref[b, 0] = (keep_ref[b] + got_ref[b].astype(jnp.float32)).astype(jnp.bfloat16)
        total = jnp.zeros((16, 1024), jnp.float32)
        for e in range(4):
            total = total + factor[0, e : e + 1, :] * own_ref[e, b, core].astype(jnp.float32)
            total = total + factor[1, e : e + 1, :] * other_ref[e, b, core].astype(jnp.float32)
        out_ref[b, 1] = total.astype(jnp.bfloat16)


def pack(sums, last, own, other, keep, got):
    return pl.pallas_call(
        pack_kernel,
        in_specs=[VM] * 6,
        out_specs=VM,
        out_shape=jax.ShapeDtypeStruct((8, 2, 16, 1024), jnp.bfloat16),
        scratch_shapes=[pltpu.VMEM((2, 4, 1024), jnp.float32)],
        compiler_params=params(12),
        cost_estimate=pl.CostEstimate(flops=4 * MIB, bytes_accessed=5 * MIB, transcendentals=0),
        name="pack",
    )(sums, last, own, other, keep, got)


def adam_kernel(
    scalars_ref, parts_ref, fresh_ref, m1_ref, m2_ref, master_ref,
    noise_out, m1_out, m2_out, master_out, weights_out,
):
    past = parts_ref[0, 0].astype(jnp.float32)
    clipped = parts_ref[0, 1].astype(jnp.float32)
    for k in range(1, 8):
        past = past + parts_ref[k, 0].astype(jnp.float32)
        clipped = clipped + parts_ref[k, 1].astype(jnp.float32)
    first = scalars_ref[0:1, 0:1]
    new_noise = (fresh_ref[...] - past) / first
    noisy = clipped + new_noise
    count = scalars_ref[1:2, 0:1]
    first_fix = 1.0 - jnp.power(jnp.float32(0.9), count)
    second_fix = 1.0 - jnp.power(jnp.float32(0.999), count)
    m1 = 0.9 * m1_ref[...] + 0.1 * noisy
    m2 = 0.999 * m2_ref[...] + 0.001 * noisy * noisy
    update = m1 / first_fix / (jnp.sqrt(m2 / second_fix) + 1e-08)
    master = master_ref[...] - 0.01 * update
    noise_out[...] = new_noise
    m1_out[...] = m1
    m2_out[...] = m2
    master_out[...] = master
    weights = master.astype(jnp.bfloat16)
    for k in range(8):
        weights_out[k] = weights


def adam(scalars, parts, fresh, moment1, moment2, master):
    row = jax.ShapeDtypeStruct(fresh.shape, jnp.float32)
    return pl.pallas_call(
        adam_kernel,
        in_specs=[VM] * 6,
        out_specs=(VM,) * 5,
        out_shape=(row, row, row, row, jax.ShapeDtypeStruct((8, 16, 1024), jnp.bfloat16)),
        compiler_params=params(8),
        cost_estimate=pl.CostEstimate(flops=MIB, bytes_accessed=2 * MIB, transcendentals=0),
        name="adam",
    )(scalars, parts, fresh, moment1, moment2, master)


def weave_kernel(own_ref, other_ref, out_ref, sems):
    core = core_index()
    a = pltpu.make_async_copy(own_ref, out_ref.at[:, core], sems.at[0])
    b = pltpu.make_async_copy(other_ref, out_ref.at[:, 1 - core], sems.at[1])
    a.start()
    b.start()
    a.wait()
    b.wait()


def weave(own, other):
    return pl.pallas_call(
        weave_kernel,
        in_specs=[HBM, HBM],
        out_specs=HBM,
        out_shape=jax.ShapeDtypeStruct((8, 2, 16, 1024), jnp.bfloat16),
        scratch_shapes=[pltpu.SemaphoreType.DMA((2,))],
        compiler_params=params(4),
        name="weave",
    )(own, other)


def shards(
    history,
    per_example,
    fresh,
    moment1,
    moment2,
    master,
    coef_table,
    table_index,
    step_number,
    cycle_slot,
):
    swap = [(i, i ^ 1) for i in range(16)]
    one_core = [[2 * k + c for k in range(8)] for c in range(2)]
    both = "param"
    across, near, far = ([(p, p ^ flip) for p in range(8)] for flip in (4, 1, 3))
    examples = per_example.reshape(4, 8, 2, 16, 1024)
    sums = place(squares(examples))
    sums = sums + lax.ppermute(sums, "slot", swap)
    weight, scalars = slot_weights(table_index, step_number, cycle_slot, coef_table)
    _, early = lax.optimization_barrier((sums, examples))
    other = lax.ppermute(early, "slot", swap)
    sums = sums + lax.ppermute(sums, both, across)
    sums, weight = lax.optimization_barrier((sums, weight))
    keep, send = past_parts(weight, history.reshape(16, 8, 2, 16, 1024), sums)
    got = lax.ppermute(send, "slot", swap)
    sums = add(sums, lax.ppermute(sums, both, near))
    sums, keep = lax.optimization_barrier((sums, keep))
    last = lax.ppermute(sums, both, far)
    packed = pack(sums, last, examples, other, keep, got)
    parts = lax.all_to_all(packed, "slot", 0, 0, tiled=True, axis_index_groups=one_core)
    new_noise, m1, m2, master_new, weights = adam(
        scalars, parts, fresh, moment1, moment2, master
    )
    gathered = lax.all_to_all(weights, "slot", 0, 0, tiled=True, axis_index_groups=one_core)
    gathered = weave(gathered, lax.ppermute(gathered, "slot", swap))
    return (new_noise, m1, m2, master_new, gathered.reshape(256, 1024))


def solution(mesh):
    placed = (
        P("slot", "param", None),
        P("slot", "param", None),
        P(("param", "slot"), None),
        P(("param", "slot"), None),
        P(("param", "slot"), None),
        P(("param", "slot"), None),
        P(),
        P(),
        P(),
        P(),
    )
    return jax.shard_map(
        shards,
        mesh=mesh,
        in_specs=placed,
        out_specs=(
            P(("param", "slot"), None),
            P(("param", "slot"), None),
            P(("param", "slot"), None),
            P(("param", "slot"), None),
            P("param", None),
        ),
        check_vma=False,
    )
```

```python
import functools

import jax
import jax.numpy as jnp
from jax import lax
from jax.experimental import pallas as pl
from jax.experimental.pallas import tpu as pltpu
from jax.sharding import PartitionSpec as P

MIB = 2**20
CORES = 2
SM = pl.BlockSpec(memory_space=pltpu.SMEM)
VM = pl.BlockSpec(memory_space=pltpu.VMEM)
HBM = pl.BlockSpec(memory_space=pl.ANY)


def params(mib):
    return pltpu.CompilerParams(vmem_limit_bytes=mib * MIB)


def core_index():
    return lax.rem(lax.axis_index("slot"), CORES)


def coef_row(coef_ref, index):
    row = lax.broadcasted_iota(jnp.int32, coef_ref.shape, 0)
    return jnp.sum(jnp.where(row == index, coef_ref[...], 0.0), axis=0, keepdims=True)


def square_kernel(grads_ref, out_ref, grads, sems):
    n = grads.shape[0]
    copies = [pltpu.make_async_copy(grads_ref.at[e], grads.at[e], sems.at[e]) for e in range(n)]
    for copy in copies:
        copy.start()
    for e in range(n):
        copies[e].wait()
        total = [jnp.zeros((16, 128), jnp.float32) for _ in range(4)]
        for r in range(16):
            for c in range(0, 1024, 128):
                x = grads[e, r // 2, r % 2, :, c : c + 128].astype(jnp.float32)
                total[(c // 128) % 4] = total[(c // 128) % 4] + x * x
        total = (total[0] + total[1]) + (total[2] + total[3])
        out_ref[e] = total[:8] + total[8:]


def squares(per_example):
    return pl.pallas_call(
        square_kernel,
        in_specs=[HBM],
        out_specs=VM,
        out_shape=jax.ShapeDtypeStruct((4, 8, 128), jnp.float32),
        scratch_shapes=[
            pltpu.VMEM(per_example.shape, per_example.dtype),
            pltpu.SemaphoreType.DMA((per_example.shape[0],)),
        ],
        compiler_params=params(8),
        cost_estimate=pl.CostEstimate(flops=1, bytes_accessed=2 * MIB, transcendentals=0),
        name="squares",
    )(pltpu.with_memory_space_constraint(per_example, pltpu.HBM))


def place_kernel(squares_ref, out_ref):
    rows = jnp.sum(squares_ref[...], axis=1)
    rows = jnp.broadcast_to(jnp.sum(rows, axis=1, keepdims=True), rows.shape)
    rows = jnp.concatenate([rows, rows], axis=0)
    core = lax.broadcasted_iota(jnp.int32, rows.shape, 0) // 4
    out_ref[...] = jnp.where(core == core_index(), rows, 0.0)


def place(sums):
    return pl.pallas_call(
        place_kernel,
        in_specs=[VM],
        out_specs=VM,
        out_shape=jax.ShapeDtypeStruct((8, 128), jnp.float32),
        compiler_params=params(4),
        cost_estimate=pl.CostEstimate(flops=2**37, bytes_accessed=2**14, transcendentals=0),
        name="place",
    )(sums)


def weights_kernel(table_ref, step_ref, cycle_ref, coef_ref, weight_ref, scalars_ref):
    slots = weight_ref.shape[0]
    coefs = coef_row(coef_ref, table_ref[0])
    first = lax.axis_index("slot") * slots
    slot = first + lax.broadcasted_iota(jnp.int32, (slots, 1), 0)
    lag = ((cycle_ref[0] - slot - 1) & 255) + 1
    lane = lax.broadcasted_iota(jnp.int32, (slots, coefs.shape[1]), 1)
    picked = jnp.sum(jnp.where(lane == lag, coefs, 0.0), axis=1, keepdims=True)
    picked = jnp.where(lag <= step_ref[0], picked, 0.0)
    weight_ref[...] = jnp.broadcast_to(picked[:, :, None], weight_ref.shape)
    row = lax.broadcasted_iota(jnp.int32, scalars_ref.shape, 0)
    count = jnp.full((1, 1), step_ref[0] + 1, jnp.int32).astype(jnp.float32)
    scalars_ref[...] = jnp.where(row == 0, coefs[:, 0:1], count)


def slot_weights(table_index, step_number, cycle_slot, coef_table):
    return pl.pallas_call(
        weights_kernel,
        in_specs=[SM] * 3 + [VM],
        out_specs=(VM, VM),
        out_shape=(
            jax.ShapeDtypeStruct((16, 8, 128), jnp.float32),
            jax.ShapeDtypeStruct((8, 128), jnp.float32),
        ),
        compiler_params=params(4),
        cost_estimate=pl.CostEstimate(flops=1, bytes_accessed=1, transcendentals=0),
        name="slot_weights",
    )(table_index, step_number, cycle_slot, coef_table)


def past_kernel(weight_ref, history_ref, _, keep_ref, send_ref):
    slots = history_ref.shape[0]
    core = core_index()
    for part, out_ref in ((1 - core, send_ref), (core, keep_ref)):

        @pl.loop(0, 8)
        def _(b, part=part, out_ref=out_ref):
            scale = [weight_ref[s] for s in range(slots)]
            for r in (0, 8):
                for c in range(0, 1024, 128):
                    total = scale[0] * history_ref[0, b, part, r : r + 8, c : c + 128]
                    for s in range(1, slots):
                        total = total + scale[s] * history_ref[s, b, part, r : r + 8, c : c + 128]
                    out_ref[b, r : r + 8, c : c + 128] = total.astype(out_ref.dtype)


def past_parts(weight, history, after):
    return pl.pallas_call(
        past_kernel,
        in_specs=[VM, VM, HBM],
        out_specs=(VM, VM),
        out_shape=(
            jax.ShapeDtypeStruct((8, 16, 1024), jnp.float32),
            jax.ShapeDtypeStruct((8, 16, 1024), jnp.bfloat16),
        ),
        compiler_params=params(4),
        cost_estimate=pl.CostEstimate(flops=1, bytes_accessed=1, transcendentals=0),
        name="past_parts",
    )(weight, history, after)


def add_kernel(a_ref, b_ref, out_ref):
    out_ref[...] = a_ref[...] + b_ref[...]


def add(a, b):
    return pl.pallas_call(
        add_kernel,
        in_specs=[VM, VM],
        out_specs=VM,
        out_shape=jax.ShapeDtypeStruct(a.shape, a.dtype),
        compiler_params=params(4),
        cost_estimate=pl.CostEstimate(flops=2**34, bytes_accessed=12288, transcendentals=0),
        name="add",
    )(a, b)


def pack_kernel(sums_ref, last_ref, own_ref, other_ref, keep_ref, got_ref, out_ref, factor):
    core = core_index()
    rms = jnp.sqrt((sums_ref[...] + last_ref[...]) / (2048.0 * 1024.0))
    one = 1.0 / jnp.maximum(rms, 1.0)
    factor[0] = jnp.broadcast_to(jnp.where(core == 0, one[0:4, 0:1], one[4:8, 0:1]), factor.shape[1:])
    factor[1] = jnp.broadcast_to(jnp.where(core == 0, one[4:8, 0:1], one[0:4, 0:1]), factor.shape[1:])

    @pl.loop(0, 8)
    def _(b):
        out_ref[b, 0] = (keep_ref[b] + got_ref[b].astype(jnp.float32)).astype(jnp.bfloat16)
        total = jnp.zeros((16, 1024), jnp.float32)
        for e in range(4):
            total = total + factor[0, e : e + 1, :] * own_ref[e, b, core].astype(jnp.float32)
            total = total + factor[1, e : e + 1, :] * other_ref[e, b, core].astype(jnp.float32)
        out_ref[b, 1] = total.astype(jnp.bfloat16)


def pack(sums, last, own, other, keep, got):
    return pl.pallas_call(
        pack_kernel,
        in_specs=[VM] * 6,
        out_specs=VM,
        out_shape=jax.ShapeDtypeStruct((8, 2, 16, 1024), jnp.bfloat16),
        scratch_shapes=[pltpu.VMEM((2, 4, 1024), jnp.float32)],
        compiler_params=params(12),
        cost_estimate=pl.CostEstimate(flops=4 * MIB, bytes_accessed=5 * MIB, transcendentals=0),
        name="pack",
    )(sums, last, own, other, keep, got)


def adam_kernel(
    scalars_ref, parts_ref, fresh_ref, m1_ref, m2_ref, master_ref,
    noise_out, m1_out, m2_out, master_out, weights_out,
):
    past = parts_ref[0, 0].astype(jnp.float32)
    clipped = parts_ref[0, 1].astype(jnp.float32)
    for k in range(1, 8):
        past = past + parts_ref[k, 0].astype(jnp.float32)
        clipped = clipped + parts_ref[k, 1].astype(jnp.float32)
    first = scalars_ref[0:1, 0:1]
    new_noise = (fresh_ref[...] - past) / first
    noisy = clipped + new_noise
    count = scalars_ref[1:2, 0:1]
    first_fix = 1.0 - jnp.power(jnp.float32(0.9), count)
    second_fix = 1.0 - jnp.power(jnp.float32(0.999), count)
    m1 = 0.9 * m1_ref[...] + 0.1 * noisy
    m2 = 0.999 * m2_ref[...] + 0.001 * noisy * noisy
    update = m1 / first_fix / (jnp.sqrt(m2 / second_fix) + 1e-08)
    master = master_ref[...] - 0.01 * update
    noise_out[...] = new_noise
    m1_out[...] = m1
    m2_out[...] = m2
    master_out[...] = master
    weights = master.astype(jnp.bfloat16)
    for k in range(8):
        weights_out[k] = weights


def adam(scalars, parts, fresh, moment1, moment2, master):
    row = jax.ShapeDtypeStruct(fresh.shape, jnp.float32)
    return pl.pallas_call(
        adam_kernel,
        in_specs=[VM] * 6,
        out_specs=(VM,) * 5,
        out_shape=(row, row, row, row, jax.ShapeDtypeStruct((8, 16, 1024), jnp.bfloat16)),
        compiler_params=params(8),
        cost_estimate=pl.CostEstimate(flops=MIB, bytes_accessed=2 * MIB, transcendentals=0),
        name="adam",
    )(scalars, parts, fresh, moment1, moment2, master)


def store_kernel(own_ref, *refs):
    rows, out_ref, stored, sems = refs[:4], refs[4], refs[5:9], refs[9]
    copies = [pltpu.make_async_copy(own_ref, out_ref.at[:, core_index()], sems.at[0])]
    for k in range(4):
        copies.append(pltpu.make_async_copy(rows[k], stored[k], sems.at[1 + k]))
    for copy in copies:
        copy.start()
    for copy in copies:
        copy.wait()


def store(own, rows):
    row = jax.ShapeDtypeStruct(rows[0].shape, rows[0].dtype)
    return pl.pallas_call(
        store_kernel,
        in_specs=[VM] * 5,
        out_specs=(HBM,) * 5,
        out_shape=(jax.ShapeDtypeStruct((8, 2, 16, 1024), jnp.bfloat16), row, row, row, row),
        scratch_shapes=[pltpu.SemaphoreType.DMA((5,))],
        compiler_params=params(4),
        cost_estimate=pl.CostEstimate(flops=1, bytes_accessed=2**20, transcendentals=0),
        name="store",
    )(own, *rows)


def weave_kernel(other_ref, _, out_ref, sem):
    copy = pltpu.make_async_copy(other_ref, out_ref.at[:, 1 - core_index()], sem)
    copy.start()
    copy.wait()


def weave(other, woven):
    return pl.pallas_call(
        weave_kernel,
        in_specs=[VM, HBM],
        out_specs=HBM,
        out_shape=jax.ShapeDtypeStruct(woven.shape, woven.dtype),
        input_output_aliases={1: 0},
        scratch_shapes=[pltpu.SemaphoreType.DMA],
        compiler_params=params(4),
        name="weave",
    )(other, woven)


def shards(
    history,
    per_example,
    fresh,
    moment1,
    moment2,
    master,
    coef_table,
    table_index,
    step_number,
    cycle_slot,
):
    swap = [(i, i ^ 1) for i in range(16)]
    one_core = [[2 * k + c for k in range(8)] for c in range(2)]
    both = "param"
    across, near, far = ([(p, p ^ flip) for p in range(8)] for flip in (4, 1, 3))
    examples = per_example.reshape(4, 8, 2, 16, 1024)
    sums = place(squares(examples))
    sums = sums + lax.ppermute(sums, "slot", swap)
    weight, scalars = slot_weights(table_index, step_number, cycle_slot, coef_table)
    _, early = lax.optimization_barrier((sums, examples))
    other = lax.ppermute(early, "slot", swap)
    sums = sums + lax.ppermute(sums, both, across)
    sums, weight = lax.optimization_barrier((sums, weight))
    keep, send = past_parts(weight, history.reshape(16, 8, 2, 16, 1024), sums)
    got = lax.ppermute(send, "slot", swap)
    sums = add(sums, lax.ppermute(sums, both, near))
    sums, keep = lax.optimization_barrier((sums, keep))
    last = lax.ppermute(sums, both, far)
    packed = pack(sums, last, examples, other, keep, got)
    parts = lax.all_to_all(packed, "slot", 0, 0, tiled=True, axis_index_groups=one_core)
    new_noise, m1, m2, master_new, weights = adam(
        scalars, parts, fresh, moment1, moment2, master
    )
    gathered = lax.all_to_all(weights, "slot", 0, 0, tiled=True, axis_index_groups=one_core)
    other_rows = lax.ppermute(gathered, "slot", swap)
    woven, *rows = store(gathered, (new_noise, m1, m2, master_new))
    return (*rows, weave(other_rows, woven).reshape(256, 1024))


def solution(mesh):
    placed = (
        P("slot", "param", None),
        P("slot", "param", None),
        P(("param", "slot"), None),
        P(("param", "slot"), None),
        P(("param", "slot"), None),
        P(("param", "slot"), None),
        P(),
        P(),
        P(),
        P(),
    )
    return jax.shard_map(
        shards,
        mesh=mesh,
        in_specs=placed,
        out_specs=(
            P(("param", "slot"), None),
            P(("param", "slot"), None),
            P(("param", "slot"), None),
            P(("param", "slot"), None),
            P("param", None),
        ),
        check_vma=False,
    )
```

```python
import functools

import jax
import jax.numpy as jnp
from jax import lax
from jax.experimental import pallas as pl
from jax.experimental.pallas import tpu as pltpu
from jax.sharding import PartitionSpec as P

MIB = 2**20
CORES = 2
SM = pl.BlockSpec(memory_space=pltpu.SMEM)
VM = pl.BlockSpec(memory_space=pltpu.VMEM)
HBM = pl.BlockSpec(memory_space=pl.ANY)


def params(mib):
    return pltpu.CompilerParams(vmem_limit_bytes=mib * MIB)


def core_index():
    return lax.rem(lax.axis_index("slot"), CORES)


def coef_row(coef_ref, index):
    row = lax.broadcasted_iota(jnp.int32, coef_ref.shape, 0)
    return jnp.sum(jnp.where(row == index, coef_ref[...], 0.0), axis=0, keepdims=True)


def square_kernel(grads_ref, out_ref, grads, sems):
    n = grads.shape[0]
    copies = [pltpu.make_async_copy(grads_ref.at[e], grads.at[e], sems.at[e]) for e in range(n)]
    for copy in copies:
        copy.start()
    for e in range(n):
        copies[e].wait()
        total = [jnp.zeros((16, 128), jnp.float32) for _ in range(4)]
        for r in range(16):
            for c in range(0, 1024, 128):
                x = grads[e, r // 2, r % 2, :, c : c + 128].astype(jnp.float32)
                total[(c // 128) % 4] = total[(c // 128) % 4] + x * x
        total = (total[0] + total[1]) + (total[2] + total[3])
        out_ref[e] = total[:8] + total[8:]


def squares(per_example):
    return pl.pallas_call(
        square_kernel,
        in_specs=[HBM],
        out_specs=VM,
        out_shape=jax.ShapeDtypeStruct((4, 8, 128), jnp.float32),
        scratch_shapes=[
            pltpu.VMEM(per_example.shape, per_example.dtype),
            pltpu.SemaphoreType.DMA((per_example.shape[0],)),
        ],
        compiler_params=params(8),
        cost_estimate=pl.CostEstimate(flops=1, bytes_accessed=2 * MIB, transcendentals=0),
        name="squares",
    )(pltpu.with_memory_space_constraint(per_example, pltpu.HBM))


def place_kernel(squares_ref, out_ref):
    rows = jnp.sum(squares_ref[...], axis=1)
    rows = jnp.broadcast_to(jnp.sum(rows, axis=1, keepdims=True), rows.shape)
    rows = jnp.concatenate([rows, rows], axis=0)
    core = lax.broadcasted_iota(jnp.int32, rows.shape, 0) // 4
    out_ref[...] = jnp.where(core == core_index(), rows, 0.0)


def place(sums):
    return pl.pallas_call(
        place_kernel,
        in_specs=[VM],
        out_specs=VM,
        out_shape=jax.ShapeDtypeStruct((8, 128), jnp.float32),
        compiler_params=params(4),
        cost_estimate=pl.CostEstimate(flops=2**37, bytes_accessed=2**14, transcendentals=0),
        name="place",
    )(sums)


def weights_kernel(table_ref, step_ref, cycle_ref, coef_ref, weight_ref, scalars_ref):
    slots = weight_ref.shape[0]
    coefs = coef_row(coef_ref, table_ref[0])
    first = lax.axis_index("slot") * slots
    slot = first + lax.broadcasted_iota(jnp.int32, (slots, 1), 0)
    lag = ((cycle_ref[0] - slot - 1) & 255) + 1
    lane = lax.broadcasted_iota(jnp.int32, (slots, coefs.shape[1]), 1)
    picked = jnp.sum(jnp.where(lane == lag, coefs, 0.0), axis=1, keepdims=True)
    picked = jnp.where(lag <= step_ref[0], picked, 0.0)
    weight_ref[...] = jnp.broadcast_to(picked[:, :, None], weight_ref.shape)
    row = lax.broadcasted_iota(jnp.int32, scalars_ref.shape, 0)
    count = jnp.full((1, 1), step_ref[0] + 1, jnp.int32).astype(jnp.float32)
    scalars_ref[...] = jnp.where(row == 0, coefs[:, 0:1], count)


def slot_weights(table_index, step_number, cycle_slot, coef_table):
    return pl.pallas_call(
        weights_kernel,
        in_specs=[SM] * 3 + [VM],
        out_specs=(VM, VM),
        out_shape=(
            jax.ShapeDtypeStruct((16, 8, 128), jnp.float32),
            jax.ShapeDtypeStruct((8, 128), jnp.float32),
        ),
        compiler_params=params(4),
        cost_estimate=pl.CostEstimate(flops=1, bytes_accessed=1, transcendentals=0),
        name="slot_weights",
    )(table_index, step_number, cycle_slot, coef_table)


def past_kernel(weight_ref, history_ref, _, keep_ref, send_ref):
    slots = history_ref.shape[0]
    core = core_index()
    for part, out_ref in ((1 - core, send_ref), (core, keep_ref)):

        @pl.loop(0, 8)
        def _(b, part=part, out_ref=out_ref):
            scale = [weight_ref[s] for s in range(slots)]
            for r in (0, 8):
                for c in range(0, 1024, 128):
                    total = scale[0] * history_ref[0, b, part, r : r + 8, c : c + 128]
                    for s in range(1, slots):
                        total = total + scale[s] * history_ref[s, b, part, r : r + 8, c : c + 128]
                    out_ref[b, r : r + 8, c : c + 128] = total.astype(out_ref.dtype)


def past_parts(weight, history, after):
    return pl.pallas_call(
        past_kernel,
        in_specs=[VM, VM, HBM],
        out_specs=(VM, VM),
        out_shape=(
            jax.ShapeDtypeStruct((8, 16, 1024), jnp.float32),
            jax.ShapeDtypeStruct((8, 16, 1024), jnp.bfloat16),
        ),
        compiler_params=params(4),
        cost_estimate=pl.CostEstimate(flops=1, bytes_accessed=1, transcendentals=0),
        name="past_parts",
    )(weight, history, after)


def add_kernel(a_ref, b_ref, out_ref):
    out_ref[...] = a_ref[...] + b_ref[...]


def add(a, b):
    return pl.pallas_call(
        add_kernel,
        in_specs=[VM, VM],
        out_specs=VM,
        out_shape=jax.ShapeDtypeStruct(a.shape, a.dtype),
        compiler_params=params(4),
        cost_estimate=pl.CostEstimate(flops=2**34, bytes_accessed=12288, transcendentals=0),
        name="add",
    )(a, b)


def factors(total):
    rms = jnp.sqrt(total / (2048.0 * 1024.0))
    return 1.0 / jnp.maximum(rms, 1.0)


def clip_kernel(sums_ref, last_ref, own_ref, keep_ref, got_ref, out_ref, past_ref, one_ref):
    core = core_index()
    one = factors(sums_ref[...] + last_ref[...])
    one_ref[...] = one
    mine = jnp.where(core == 0, one[0:4], one[4:8])
    scale = [jnp.broadcast_to(mine[e : e + 1], (16, 128)) for e in range(4)]

    @pl.loop(0, 8)
    def _(b):
        past_ref[b] = (keep_ref[b] + got_ref[b].astype(jnp.float32)).astype(jnp.bfloat16)
        for c in range(0, 1024, 128):
            total = scale[0] * own_ref[0, b, core, :, c : c + 128].astype(jnp.float32)
            for e in range(1, 4):
                total = total + scale[e] * own_ref[e, b, core, :, c : c + 128].astype(jnp.float32)
            out_ref[b, :, c : c + 128] = total


def clip(sums, last, own, keep, got):
    return pl.pallas_call(
        clip_kernel,
        in_specs=[VM] * 5,
        out_specs=(VM, VM, VM),
        out_shape=(
            jax.ShapeDtypeStruct((8, 16, 1024), jnp.float32),
            jax.ShapeDtypeStruct((8, 16, 1024), jnp.bfloat16),
            jax.ShapeDtypeStruct((8, 128), jnp.float32),
        ),
        compiler_params=params(12),
        cost_estimate=pl.CostEstimate(flops=2**33, bytes_accessed=1, transcendentals=0),
        name="clip",
    )(sums, last, own, keep, got)


def pack_kernel(own_ref, past_ref, one_ref, other_ref, out_ref):
    core = core_index()
    one = one_ref[...]
    other = jnp.where(core == 0, one[4:8], one[0:4])
    scale = [jnp.broadcast_to(other[e : e + 1], (16, 128)) for e in range(4)]

    @pl.loop(0, 8)
    def _(b):
        out_ref[b, 0] = past_ref[b]
        for c in range(0, 1024, 128):
            total = own_ref[b, :, c : c + 128]
            for e in range(4):
                total = total + scale[e] * other_ref[e, b, core, :, c : c + 128].astype(jnp.float32)
            out_ref[b, 1, :, c : c + 128] = total.astype(jnp.bfloat16)


def pack(clipped, past, one, other):
    return pl.pallas_call(
        pack_kernel,
        in_specs=[VM] * 4,
        out_specs=VM,
        out_shape=jax.ShapeDtypeStruct((8, 2, 16, 1024), jnp.bfloat16),
        compiler_params=params(12),
        cost_estimate=pl.CostEstimate(flops=1, bytes_accessed=1, transcendentals=0),
        name="pack",
    )(clipped, past, one, other)


def adam_kernel(
    scalars_ref, parts_ref, fresh_ref, m1_ref, m2_ref, master_ref,
    noise_out, m1_out, m2_out, master_out, weights_out,
):
    past = parts_ref[0, 0].astype(jnp.float32)
    clipped = parts_ref[0, 1].astype(jnp.float32)
    for k in range(1, 8):
        past = past + parts_ref[k, 0].astype(jnp.float32)
        clipped = clipped + parts_ref[k, 1].astype(jnp.float32)
    first = scalars_ref[0:1, 0:1]
    new_noise = (fresh_ref[...] - past) / first
    noisy = clipped + new_noise
    count = scalars_ref[1:2, 0:1]
    first_fix = 1.0 - jnp.power(jnp.float32(0.9), count)
    second_fix = 1.0 - jnp.power(jnp.float32(0.999), count)
    m1 = 0.9 * m1_ref[...] + 0.1 * noisy
    m2 = 0.999 * m2_ref[...] + 0.001 * noisy * noisy
    update = m1 / first_fix / (jnp.sqrt(m2 / second_fix) + 1e-08)
    master = master_ref[...] - 0.01 * update
    noise_out[...] = new_noise
    m1_out[...] = m1
    m2_out[...] = m2
    master_out[...] = master
    weights = master.astype(jnp.bfloat16)
    for k in range(8):
        weights_out[k] = weights


def adam(scalars, parts, fresh, moment1, moment2, master):
    row = jax.ShapeDtypeStruct(fresh.shape, jnp.float32)
    return pl.pallas_call(
        adam_kernel,
        in_specs=[VM] * 6,
        out_specs=(VM,) * 5,
        out_shape=(row, row, row, row, jax.ShapeDtypeStruct((8, 16, 1024), jnp.bfloat16)),
        compiler_params=params(8),
        cost_estimate=pl.CostEstimate(flops=MIB, bytes_accessed=2 * MIB, transcendentals=0),
        name="adam",
    )(scalars, parts, fresh, moment1, moment2, master)


def store_kernel(own_ref, *refs):
    rows, out_ref, stored, sems = refs[:4], refs[4], refs[5:9], refs[9]
    copies = [pltpu.make_async_copy(own_ref, out_ref.at[:, core_index()], sems.at[0])]
    for k in range(4):
        copies.append(pltpu.make_async_copy(rows[k], stored[k], sems.at[1 + k]))
    for copy in copies:
        copy.start()
    for copy in copies:
        copy.wait()


def store(own, rows):
    row = jax.ShapeDtypeStruct(rows[0].shape, rows[0].dtype)
    return pl.pallas_call(
        store_kernel,
        in_specs=[VM] * 5,
        out_specs=(HBM,) * 5,
        out_shape=(jax.ShapeDtypeStruct((8, 2, 16, 1024), jnp.bfloat16), row, row, row, row),
        scratch_shapes=[pltpu.SemaphoreType.DMA((5,))],
        compiler_params=params(4),
        cost_estimate=pl.CostEstimate(flops=1, bytes_accessed=2**20, transcendentals=0),
        name="store",
    )(own, *rows)


def weave_kernel(other_ref, _, out_ref, sem):
    copy = pltpu.make_async_copy(other_ref, out_ref.at[:, 1 - core_index()], sem)
    copy.start()
    copy.wait()


def weave(other, woven):
    return pl.pallas_call(
        weave_kernel,
        in_specs=[VM, HBM],
        out_specs=HBM,
        out_shape=jax.ShapeDtypeStruct(woven.shape, woven.dtype),
        input_output_aliases={1: 0},
        scratch_shapes=[pltpu.SemaphoreType.DMA],
        compiler_params=params(4),
        name="weave",
    )(other, woven)


def shards(
    history,
    per_example,
    fresh,
    moment1,
    moment2,
    master,
    coef_table,
    table_index,
    step_number,
    cycle_slot,
):
    swap = [(i, i ^ 1) for i in range(16)]
    one_core = [[2 * k + c for k in range(8)] for c in range(2)]
    both = "param"
    across, near, far = ([(p, p ^ flip) for p in range(8)] for flip in (4, 1, 3))
    examples = per_example.reshape(4, 8, 2, 16, 1024)
    sums = place(squares(examples))
    sums = sums + lax.ppermute(sums, "slot", swap)
    weight, scalars = slot_weights(table_index, step_number, cycle_slot, coef_table)
    _, early = lax.optimization_barrier((sums, examples))
    other = lax.ppermute(early, "slot", swap)
    sums = sums + lax.ppermute(sums, both, across)
    sums, weight = lax.optimization_barrier((sums, weight))
    keep, send = past_parts(weight, history.reshape(16, 8, 2, 16, 1024), sums)
    got = lax.ppermute(send, "slot", swap)
    sums = add(sums, lax.ppermute(sums, both, near))
    sums, keep = lax.optimization_barrier((sums, keep))
    last = lax.ppermute(sums, both, far)
    packed = pack(*clip(sums, last, examples, keep, got), other)
    parts = lax.all_to_all(packed, "slot", 0, 0, tiled=True, axis_index_groups=one_core)
    new_noise, m1, m2, master_new, weights = adam(
        scalars, parts, fresh, moment1, moment2, master
    )
    gathered = lax.all_to_all(weights, "slot", 0, 0, tiled=True, axis_index_groups=one_core)
    other_rows = lax.ppermute(gathered, "slot", swap)
    woven, *rows = store(gathered, (new_noise, m1, m2, master_new))
    return (*rows, weave(other_rows, woven).reshape(256, 1024))


def solution(mesh):
    placed = (
        P("slot", "param", None),
        P("slot", "param", None),
        P(("param", "slot"), None),
        P(("param", "slot"), None),
        P(("param", "slot"), None),
        P(("param", "slot"), None),
        P(),
        P(),
        P(),
        P(),
    )
    return jax.shard_map(
        shards,
        mesh=mesh,
        in_specs=placed,
        out_specs=(
            P(("param", "slot"), None),
            P(("param", "slot"), None),
            P(("param", "slot"), None),
            P(("param", "slot"), None),
            P("param", None),
        ),
        check_vma=False,
    )
```

```python
import functools

import jax
import jax.numpy as jnp
from jax import lax
from jax.experimental import pallas as pl
from jax.experimental.pallas import tpu as pltpu
from jax.sharding import PartitionSpec as P

MIB = 2**20
CORES = 2
SM = pl.BlockSpec(memory_space=pltpu.SMEM)
VM = pl.BlockSpec(memory_space=pltpu.VMEM)
HBM = pl.BlockSpec(memory_space=pl.ANY)


def params(mib):
    return pltpu.CompilerParams(vmem_limit_bytes=mib * MIB)


def core_index():
    return lax.rem(lax.axis_index("slot"), CORES)


def coef_row(coef_ref, index):
    row = lax.broadcasted_iota(jnp.int32, coef_ref.shape, 0)
    return jnp.sum(jnp.where(row == index, coef_ref[...], 0.0), axis=0, keepdims=True)


def square_kernel(grads_ref, out_ref, grads, sems):
    n = grads.shape[0]
    copies = [pltpu.make_async_copy(grads_ref.at[e], grads.at[e], sems.at[e]) for e in range(n)]
    for copy in copies:
        copy.start()
    for e in range(n):
        copies[e].wait()
        total = [jnp.zeros((16, 128), jnp.float32) for _ in range(4)]
        for r in range(16):
            for c in range(0, 1024, 128):
                x = grads[e, r // 2, r % 2, :, c : c + 128].astype(jnp.float32)
                total[(c // 128) % 4] = total[(c // 128) % 4] + x * x
        total = (total[0] + total[1]) + (total[2] + total[3])
        out_ref[e] = total[:8] + total[8:]


def squares(per_example):
    return pl.pallas_call(
        square_kernel,
        in_specs=[HBM],
        out_specs=VM,
        out_shape=jax.ShapeDtypeStruct((4, 8, 128), jnp.float32),
        scratch_shapes=[
            pltpu.VMEM(per_example.shape, per_example.dtype),
            pltpu.SemaphoreType.DMA((per_example.shape[0],)),
        ],
        compiler_params=params(8),
        cost_estimate=pl.CostEstimate(flops=1, bytes_accessed=2 * MIB, transcendentals=0),
        name="squares",
    )(pltpu.with_memory_space_constraint(per_example, pltpu.HBM))


def place_kernel(squares_ref, out_ref):
    rows = jnp.sum(squares_ref[...], axis=1)
    rows = jnp.broadcast_to(jnp.sum(rows, axis=1, keepdims=True), rows.shape)
    rows = jnp.concatenate([rows, rows], axis=0)
    core = lax.broadcasted_iota(jnp.int32, rows.shape, 0) // 4
    out_ref[...] = jnp.where(core == core_index(), rows, 0.0)


def place(sums):
    return pl.pallas_call(
        place_kernel,
        in_specs=[VM],
        out_specs=VM,
        out_shape=jax.ShapeDtypeStruct((8, 128), jnp.float32),
        compiler_params=params(4),
        cost_estimate=pl.CostEstimate(flops=2**37, bytes_accessed=2**14, transcendentals=0),
        name="place",
    )(sums)


def weights_kernel(table_ref, step_ref, cycle_ref, coef_ref, weight_ref, scalars_ref):
    slots = weight_ref.shape[0]
    coefs = coef_row(coef_ref, table_ref[0])
    first = lax.axis_index("slot") * slots
    slot = first + lax.broadcasted_iota(jnp.int32, (slots, 1), 0)
    lag = ((cycle_ref[0] - slot - 1) & 255) + 1
    lane = lax.broadcasted_iota(jnp.int32, (slots, coefs.shape[1]), 1)
    picked = jnp.sum(jnp.where(lane == lag, coefs, 0.0), axis=1, keepdims=True)
    picked = jnp.where(lag <= step_ref[0], picked, 0.0)
    weight_ref[...] = jnp.broadcast_to(picked[:, :, None], weight_ref.shape)
    row = lax.broadcasted_iota(jnp.int32, scalars_ref.shape, 0)
    count = jnp.full((1, 1), step_ref[0] + 1, jnp.int32).astype(jnp.float32)
    scalars_ref[...] = jnp.where(row == 0, coefs[:, 0:1], count)


def slot_weights(table_index, step_number, cycle_slot, coef_table):
    return pl.pallas_call(
        weights_kernel,
        in_specs=[SM] * 3 + [VM],
        out_specs=(VM, VM),
        out_shape=(
            jax.ShapeDtypeStruct((16, 8, 128), jnp.float32),
            jax.ShapeDtypeStruct((8, 128), jnp.float32),
        ),
        compiler_params=params(4),
        cost_estimate=pl.CostEstimate(flops=1, bytes_accessed=1, transcendentals=0),
        name="slot_weights",
    )(table_index, step_number, cycle_slot, coef_table)


def past_kernel(weight_ref, history_ref, _, keep_ref, send_ref):
    slots = history_ref.shape[0]
    core = core_index()
    for part, out_ref in ((1 - core, send_ref), (core, keep_ref)):

        @pl.loop(0, 8)
        def _(b, part=part, out_ref=out_ref):
            scale = [weight_ref[s] for s in range(slots)]
            for c in range(0, 1024, 128):
                halves = []
                for r in (0, 8):
                    total = scale[0] * history_ref[0, b, part, r : r + 8, c : c + 128]
                    for s in range(1, slots):
                        total = total + scale[s] * history_ref[s, b, part, r : r + 8, c : c + 128]
                    halves.append(total)
                out_ref[b, :, c : c + 128] = jnp.concatenate(halves, axis=0).astype(out_ref.dtype)


def past_parts(weight, history, after):
    return pl.pallas_call(
        past_kernel,
        in_specs=[VM, VM, HBM],
        out_specs=(VM, VM),
        out_shape=(
            jax.ShapeDtypeStruct((8, 16, 1024), jnp.float32),
            jax.ShapeDtypeStruct((8, 16, 1024), jnp.bfloat16),
        ),
        compiler_params=params(4),
        cost_estimate=pl.CostEstimate(flops=1, bytes_accessed=1, transcendentals=0),
        name="past_parts",
    )(weight, history, after)


def add_kernel(a_ref, b_ref, out_ref):
    out_ref[...] = a_ref[...] + b_ref[...]


def add(a, b):
    return pl.pallas_call(
        add_kernel,
        in_specs=[VM, VM],
        out_specs=VM,
        out_shape=jax.ShapeDtypeStruct(a.shape, a.dtype),
        compiler_params=params(4),
        cost_estimate=pl.CostEstimate(flops=2**34, bytes_accessed=12288, transcendentals=0),
        name="add",
    )(a, b)


def factors(total):
    rms = jnp.sqrt(total / (2048.0 * 1024.0))
    return 1.0 / jnp.maximum(rms, 1.0)


def clip_kernel(sums_ref, last_ref, own_ref, keep_ref, got_ref, out_ref, past_ref, one_ref):
    core = core_index()
    one = factors(sums_ref[...] + last_ref[...])
    one_ref[...] = one
    mine = jnp.where(core == 0, one[0:4], one[4:8])
    scale = [jnp.broadcast_to(mine[e : e + 1], (16, 128)) for e in range(4)]

    @pl.loop(0, 8)
    def _(b):
        past_ref[b] = (keep_ref[b] + got_ref[b].astype(jnp.float32)).astype(jnp.bfloat16)
        for c in range(0, 1024, 128):
            total = scale[0] * own_ref[0, b, core, :, c : c + 128].astype(jnp.float32)
            for e in range(1, 4):
                total = total + scale[e] * own_ref[e, b, core, :, c : c + 128].astype(jnp.float32)
            out_ref[b, :, c : c + 128] = total


def clip(sums, last, own, keep, got):
    return pl.pallas_call(
        clip_kernel,
        in_specs=[VM] * 5,
        out_specs=(VM, VM, VM),
        out_shape=(
            jax.ShapeDtypeStruct((8, 16, 1024), jnp.float32),
            jax.ShapeDtypeStruct((8, 16, 1024), jnp.bfloat16),
            jax.ShapeDtypeStruct((8, 128), jnp.float32),
        ),
        compiler_params=params(12),
        cost_estimate=pl.CostEstimate(flops=2**33, bytes_accessed=1, transcendentals=0),
        name="clip",
    )(sums, last, own, keep, got)


def pack_kernel(own_ref, past_ref, one_ref, other_ref, out_ref):
    core = core_index()
    one = one_ref[...]
    other = jnp.where(core == 0, one[4:8], one[0:4])
    scale = [jnp.broadcast_to(other[e : e + 1], (16, 128)) for e in range(4)]

    @pl.loop(0, 8)
    def _(b):
        out_ref[b, 0] = past_ref[b]
        for c in range(0, 1024, 128):
            total = own_ref[b, :, c : c + 128]
            for e in range(4):
                total = total + scale[e] * other_ref[e, b, core, :, c : c + 128].astype(jnp.float32)
            out_ref[b, 1, :, c : c + 128] = total.astype(jnp.bfloat16)


def pack(clipped, past, one, other):
    return pl.pallas_call(
        pack_kernel,
        in_specs=[VM] * 4,
        out_specs=VM,
        out_shape=jax.ShapeDtypeStruct((8, 2, 16, 1024), jnp.bfloat16),
        compiler_params=params(12),
        cost_estimate=pl.CostEstimate(flops=1, bytes_accessed=1, transcendentals=0),
        name="pack",
    )(clipped, past, one, other)


def adam_kernel(
    scalars_ref, parts_ref, fresh_ref, m1_ref, m2_ref, master_ref,
    noise_out, m1_out, m2_out, master_out, weights_out,
):
    past = parts_ref[0, 0].astype(jnp.float32)
    clipped = parts_ref[0, 1].astype(jnp.float32)
    for k in range(1, 8):
        past = past + parts_ref[k, 0].astype(jnp.float32)
        clipped = clipped + parts_ref[k, 1].astype(jnp.float32)
    first = scalars_ref[0:1, 0:1]
    new_noise = (fresh_ref[...] - past) / first
    noisy = clipped + new_noise
    count = scalars_ref[1:2, 0:1]
    first_fix = 1.0 - jnp.power(jnp.float32(0.9), count)
    second_fix = 1.0 - jnp.power(jnp.float32(0.999), count)
    m1 = 0.9 * m1_ref[...] + 0.1 * noisy
    m2 = 0.999 * m2_ref[...] + 0.001 * noisy * noisy
    update = m1 / first_fix / (jnp.sqrt(m2 / second_fix) + 1e-08)
    master = master_ref[...] - 0.01 * update
    noise_out[...] = new_noise
    m1_out[...] = m1
    m2_out[...] = m2
    master_out[...] = master
    weights = master.astype(jnp.bfloat16)
    for k in range(8):
        weights_out[k] = weights


def adam(scalars, parts, fresh, moment1, moment2, master):
    row = jax.ShapeDtypeStruct(fresh.shape, jnp.float32)
    return pl.pallas_call(
        adam_kernel,
        in_specs=[VM] * 6,
        out_specs=(VM,) * 5,
        out_shape=(row, row, row, row, jax.ShapeDtypeStruct((8, 16, 1024), jnp.bfloat16)),
        compiler_params=params(8),
        cost_estimate=pl.CostEstimate(flops=MIB, bytes_accessed=2 * MIB, transcendentals=0),
        name="adam",
    )(scalars, parts, fresh, moment1, moment2, master)


def store_kernel(own_ref, *refs):
    rows, out_ref, stored, sems = refs[:4], refs[4], refs[5:9], refs[9]
    copies = [pltpu.make_async_copy(own_ref, out_ref.at[:, core_index()], sems.at[0])]
    for k in range(4):
        copies.append(pltpu.make_async_copy(rows[k], stored[k], sems.at[1 + k]))
    for copy in copies:
        copy.start()
    for copy in copies:
        copy.wait()


def store(own, rows):
    row = jax.ShapeDtypeStruct(rows[0].shape, rows[0].dtype)
    return pl.pallas_call(
        store_kernel,
        in_specs=[VM] * 5,
        out_specs=(HBM,) * 5,
        out_shape=(jax.ShapeDtypeStruct((8, 2, 16, 1024), jnp.bfloat16), row, row, row, row),
        scratch_shapes=[pltpu.SemaphoreType.DMA((5,))],
        compiler_params=params(4),
        cost_estimate=pl.CostEstimate(flops=1, bytes_accessed=2**20, transcendentals=0),
        name="store",
    )(own, *rows)


def weave_kernel(other_ref, _, out_ref, sem):
    copy = pltpu.make_async_copy(other_ref, out_ref.at[:, 1 - core_index()], sem)
    copy.start()
    copy.wait()


def weave(other, woven):
    return pl.pallas_call(
        weave_kernel,
        in_specs=[VM, HBM],
        out_specs=HBM,
        out_shape=jax.ShapeDtypeStruct(woven.shape, woven.dtype),
        input_output_aliases={1: 0},
        scratch_shapes=[pltpu.SemaphoreType.DMA],
        compiler_params=params(4),
        name="weave",
    )(other, woven)


def shards(
    history,
    per_example,
    fresh,
    moment1,
    moment2,
    master,
    coef_table,
    table_index,
    step_number,
    cycle_slot,
):
    swap = [(i, i ^ 1) for i in range(16)]
    one_core = [[2 * k + c for k in range(8)] for c in range(2)]
    both = "param"
    across, near, far = ([(p, p ^ flip) for p in range(8)] for flip in (4, 1, 3))
    examples = per_example.reshape(4, 8, 2, 16, 1024)
    sums = place(squares(examples))
    sums = sums + lax.ppermute(sums, "slot", swap)
    weight, scalars = slot_weights(table_index, step_number, cycle_slot, coef_table)
    _, early = lax.optimization_barrier((sums, examples))
    other = lax.ppermute(early, "slot", swap)
    sums = sums + lax.ppermute(sums, both, far)
    sums, weight = lax.optimization_barrier((sums, weight))
    keep, send = past_parts(weight, history.reshape(16, 8, 2, 16, 1024), sums)
    got = lax.ppermute(send, "slot", swap)
    sums = add(sums, lax.ppermute(sums, both, near))
    sums, keep = lax.optimization_barrier((sums, keep))
    last = lax.ppermute(sums, both, across)
    packed = pack(*clip(sums, last, examples, keep, got), other)
    parts = lax.all_to_all(packed, "slot", 0, 0, tiled=True, axis_index_groups=one_core)
    new_noise, m1, m2, master_new, weights = adam(
        scalars, parts, fresh, moment1, moment2, master
    )
    gathered = lax.all_to_all(weights, "slot", 0, 0, tiled=True, axis_index_groups=one_core)
    other_rows = lax.ppermute(gathered, "slot", swap)
    woven, *rows = store(gathered, (new_noise, m1, m2, master_new))
    return (*rows, weave(other_rows, woven).reshape(256, 1024))


def solution(mesh):
    placed = (
        P("slot", "param", None),
        P("slot", "param", None),
        P(("param", "slot"), None),
        P(("param", "slot"), None),
        P(("param", "slot"), None),
        P(("param", "slot"), None),
        P(),
        P(),
        P(),
        P(),
    )
    return jax.shard_map(
        shards,
        mesh=mesh,
        in_specs=placed,
        out_specs=(
            P(("param", "slot"), None),
            P(("param", "slot"), None),
            P(("param", "slot"), None),
            P(("param", "slot"), None),
            P("param", None),
        ),
        check_vma=False,
    )
```

```python
import functools

import jax
import jax.numpy as jnp
from jax import lax
from jax.experimental import pallas as pl
from jax.experimental.pallas import tpu as pltpu
from jax.sharding import PartitionSpec as P

MIB = 2**20
CORES = 2
SM = pl.BlockSpec(memory_space=pltpu.SMEM)
VM = pl.BlockSpec(memory_space=pltpu.VMEM)
HBM = pl.BlockSpec(memory_space=pl.ANY)


def params(mib):
    return pltpu.CompilerParams(vmem_limit_bytes=mib * MIB)


def core_index():
    return lax.rem(lax.axis_index("slot"), CORES)


def coef_row(coef_ref, index):
    row = lax.broadcasted_iota(jnp.int32, coef_ref.shape, 0)
    return jnp.sum(jnp.where(row == index, coef_ref[...], 0.0), axis=0, keepdims=True)


def square_kernel(grads_ref, out_ref, grads, sems):
    n = grads.shape[0]
    copies = [pltpu.make_async_copy(grads_ref.at[e], grads.at[e], sems.at[e]) for e in range(n)]
    for copy in copies:
        copy.start()
    for e in range(n):
        copies[e].wait()
        total = [jnp.zeros((16, 128), jnp.float32) for _ in range(4)]
        for r in range(16):
            for c in range(0, 1024, 128):
                x = grads[e, r // 2, r % 2, :, c : c + 128].astype(jnp.float32)
                total[(c // 128) % 4] = total[(c // 128) % 4] + x * x
        total = (total[0] + total[1]) + (total[2] + total[3])
        out_ref[e] = total[:8] + total[8:]


def squares(per_example):
    return pl.pallas_call(
        square_kernel,
        in_specs=[HBM],
        out_specs=VM,
        out_shape=jax.ShapeDtypeStruct((4, 8, 128), jnp.float32),
        scratch_shapes=[
            pltpu.VMEM(per_example.shape, per_example.dtype),
            pltpu.SemaphoreType.DMA((per_example.shape[0],)),
        ],
        compiler_params=params(8),
        cost_estimate=pl.CostEstimate(flops=1, bytes_accessed=2 * MIB, transcendentals=0),
        name="squares",
    )(pltpu.with_memory_space_constraint(per_example, pltpu.HBM))


def place_kernel(squares_ref, out_ref):
    rows = jnp.sum(squares_ref[...], axis=1)
    rows = jnp.broadcast_to(jnp.sum(rows, axis=1, keepdims=True), rows.shape)
    rows = jnp.concatenate([rows, rows], axis=0)
    core = lax.broadcasted_iota(jnp.int32, rows.shape, 0) // 4
    out_ref[...] = jnp.where(core == core_index(), rows, 0.0)


def place(sums):
    return pl.pallas_call(
        place_kernel,
        in_specs=[VM],
        out_specs=VM,
        out_shape=jax.ShapeDtypeStruct((8, 128), jnp.float32),
        compiler_params=params(4),
        cost_estimate=pl.CostEstimate(flops=2**37, bytes_accessed=2**14, transcendentals=0),
        name="place",
    )(sums)


def weights_kernel(table_ref, step_ref, cycle_ref, coef_ref, weight_ref, scalars_ref):
    slots = weight_ref.shape[0]
    coefs = coef_row(coef_ref, table_ref[0])
    first = lax.axis_index("slot") * slots
    slot = first + lax.broadcasted_iota(jnp.int32, (slots, 1), 0)
    lag = ((cycle_ref[0] - slot - 1) & 255) + 1
    lane = lax.broadcasted_iota(jnp.int32, (slots, coefs.shape[1]), 1)
    picked = jnp.sum(jnp.where(lane == lag, coefs, 0.0), axis=1, keepdims=True)
    picked = jnp.where(lag <= step_ref[0], picked, 0.0)
    weight_ref[...] = jnp.broadcast_to(picked[:, :, None], weight_ref.shape)
    row = lax.broadcasted_iota(jnp.int32, scalars_ref.shape, 0)
    count = jnp.full((1, 1), step_ref[0] + 1, jnp.int32).astype(jnp.float32)
    scalars_ref[...] = jnp.where(row == 0, coefs[:, 0:1], count)


def slot_weights(table_index, step_number, cycle_slot, coef_table):
    return pl.pallas_call(
        weights_kernel,
        in_specs=[SM] * 3 + [VM],
        out_specs=(VM, VM),
        out_shape=(
            jax.ShapeDtypeStruct((16, 8, 128), jnp.float32),
            jax.ShapeDtypeStruct((8, 128), jnp.float32),
        ),
        compiler_params=params(4),
        cost_estimate=pl.CostEstimate(flops=1, bytes_accessed=1, transcendentals=0),
        name="slot_weights",
    )(table_index, step_number, cycle_slot, coef_table)


def past_kernel(weight_ref, history_ref, _, keep_ref, send_ref):
    slots = history_ref.shape[0]
    core = core_index()
    for part, out_ref in ((1 - core, send_ref), (core, keep_ref)):

        @pl.loop(0, 8)
        def _(b, part=part, out_ref=out_ref):
            scale = [weight_ref[s] for s in range(slots)]
            for c in range(0, 1024, 128):
                halves = []
                for r in (0, 8):
                    total = scale[0] * history_ref[0, b, part, r : r + 8, c : c + 128]
                    for s in range(1, slots):
                        total = total + scale[s] * history_ref[s, b, part, r : r + 8, c : c + 128]
                    halves.append(total)
                out_ref[b, :, c : c + 128] = jnp.concatenate(halves, axis=0).astype(out_ref.dtype)


def past_parts(weight, history, after):
    return pl.pallas_call(
        past_kernel,
        in_specs=[VM, VM, HBM],
        out_specs=(VM, VM),
        out_shape=(
            jax.ShapeDtypeStruct((8, 16, 1024), jnp.float32),
            jax.ShapeDtypeStruct((8, 16, 1024), jnp.bfloat16),
        ),
        compiler_params=params(4),
        cost_estimate=pl.CostEstimate(flops=1, bytes_accessed=1, transcendentals=0),
        name="past_parts",
    )(weight, history, after)


def add_kernel(a_ref, b_ref, out_ref):
    out_ref[...] = a_ref[...] + b_ref[...]


def add(a, b):
    return pl.pallas_call(
        add_kernel,
        in_specs=[VM, VM],
        out_specs=VM,
        out_shape=jax.ShapeDtypeStruct(a.shape, a.dtype),
        compiler_params=params(4),
        cost_estimate=pl.CostEstimate(flops=2**34, bytes_accessed=12288, transcendentals=0),
        name="add",
    )(a, b)


def factors(total):
    rms = jnp.sqrt(total / (2048.0 * 1024.0))
    return 1.0 / jnp.maximum(rms, 1.0)


def clip_kernel(sums_ref, last_ref, own_ref, keep_ref, got_ref, out_ref, past_ref, one_ref):
    core = core_index()
    one = factors(sums_ref[...] + last_ref[...])
    one_ref[...] = one
    mine = jnp.where(core == 0, one[0:4], one[4:8])
    scale = [jnp.broadcast_to(mine[e : e + 1], (16, 128)) for e in range(4)]

    @pl.loop(0, 8)
    def _(b):
        past_ref[b] = (keep_ref[b] + got_ref[b].astype(jnp.float32)).astype(jnp.bfloat16)
        for c in range(0, 1024, 128):
            total = scale[0] * own_ref[0, b, core, :, c : c + 128].astype(jnp.float32)
            for e in range(1, 4):
                total = total + scale[e] * own_ref[e, b, core, :, c : c + 128].astype(jnp.float32)
            out_ref[b, :, c : c + 128] = total


def clip(sums, last, own, keep, got):
    return pl.pallas_call(
        clip_kernel,
        in_specs=[VM] * 5,
        out_specs=(VM, VM, VM),
        out_shape=(
            jax.ShapeDtypeStruct((8, 16, 1024), jnp.float32),
            jax.ShapeDtypeStruct((8, 16, 1024), jnp.bfloat16),
            jax.ShapeDtypeStruct((8, 128), jnp.float32),
        ),
        compiler_params=params(12),
        cost_estimate=pl.CostEstimate(flops=2**33, bytes_accessed=1, transcendentals=0),
        name="clip",
    )(sums, last, own, keep, got)


def pack_kernel(own_ref, past_ref, one_ref, other_ref, out_ref):
    core = core_index()
    one = one_ref[...]
    other = jnp.where(core == 0, one[4:8], one[0:4])
    scale = [jnp.broadcast_to(other[e : e + 1], (16, 128)) for e in range(4)]

    @pl.loop(0, 8)
    def _(b):
        out_ref[b, 0] = past_ref[b]
        for c in range(0, 1024, 128):
            total = own_ref[b, :, c : c + 128]
            for e in range(4):
                total = total + scale[e] * other_ref[e, b, core, :, c : c + 128].astype(jnp.float32)
            out_ref[b, 1, :, c : c + 128] = total.astype(jnp.bfloat16)


def pack(clipped, past, one, other):
    return pl.pallas_call(
        pack_kernel,
        in_specs=[VM] * 4,
        out_specs=VM,
        out_shape=jax.ShapeDtypeStruct((8, 2, 16, 1024), jnp.bfloat16),
        compiler_params=params(12),
        cost_estimate=pl.CostEstimate(flops=1, bytes_accessed=1, transcendentals=0),
        name="pack",
    )(clipped, past, one, other)


def adam_kernel(
    scalars_ref, parts_ref, fresh_ref, m1_ref, m2_ref, master_ref,
    noise_out, m1_out, m2_out, master_out, weights_out,
):
    past = parts_ref[0, 0].astype(jnp.float32)
    clipped = parts_ref[0, 1].astype(jnp.float32)
    for k in range(1, 8):
        past = past + parts_ref[k, 0].astype(jnp.float32)
        clipped = clipped + parts_ref[k, 1].astype(jnp.float32)
    first = scalars_ref[0:1, 0:1]
    new_noise = (fresh_ref[...] - past) / first
    noisy = clipped + new_noise
    count = scalars_ref[1:2, 0:1]
    first_fix = 1.0 - jnp.power(jnp.float32(0.9), count)
    second_fix = 1.0 - jnp.power(jnp.float32(0.999), count)
    m1 = 0.9 * m1_ref[...] + 0.1 * noisy
    m2 = 0.999 * m2_ref[...] + 0.001 * noisy * noisy
    update = m1 / first_fix / (jnp.sqrt(m2 / second_fix) + 1e-08)
    master = master_ref[...] - 0.01 * update
    noise_out[...] = new_noise
    m1_out[...] = m1
    m2_out[...] = m2
    master_out[...] = master
    weights = master.astype(jnp.bfloat16)
    for k in range(8):
        weights_out[k] = weights


def adam(scalars, parts, fresh, moment1, moment2, master):
    row = jax.ShapeDtypeStruct(fresh.shape, jnp.float32)
    return pl.pallas_call(
        adam_kernel,
        in_specs=[VM] * 6,
        out_specs=(VM,) * 5,
        out_shape=(row, row, row, row, jax.ShapeDtypeStruct((8, 16, 1024), jnp.bfloat16)),
        compiler_params=params(8),
        cost_estimate=pl.CostEstimate(flops=MIB, bytes_accessed=2 * MIB, transcendentals=0),
        name="adam",
    )(scalars, parts, fresh, moment1, moment2, master)


def store_kernel(own_ref, *refs):
    rows, out_ref, stored, sems = refs[:4], refs[4], refs[5:9], refs[9]
    copies = [pltpu.make_async_copy(own_ref, out_ref.at[:, core_index()], sems.at[0])]
    for k in range(4):
        copies.append(pltpu.make_async_copy(rows[k], stored[k], sems.at[1 + k]))
    for copy in copies:
        copy.start()
    for copy in copies:
        copy.wait()


def store(own, rows):
    row = jax.ShapeDtypeStruct(rows[0].shape, rows[0].dtype)
    return pl.pallas_call(
        store_kernel,
        in_specs=[VM] * 5,
        out_specs=(HBM,) * 5,
        out_shape=(jax.ShapeDtypeStruct((8, 2, 16, 1024), jnp.bfloat16), row, row, row, row),
        scratch_shapes=[pltpu.SemaphoreType.DMA((5,))],
        compiler_params=params(4),
        cost_estimate=pl.CostEstimate(flops=1, bytes_accessed=2**20, transcendentals=0),
        name="store",
    )(own, *rows)


def weave_kernel(other_ref, _, out_ref, sem):
    copy = pltpu.make_async_copy(other_ref, out_ref.at[:, 1 - core_index()], sem)
    copy.start()
    copy.wait()


def weave(other, woven):
    return pl.pallas_call(
        weave_kernel,
        in_specs=[VM, HBM],
        out_specs=HBM,
        out_shape=jax.ShapeDtypeStruct(woven.shape, woven.dtype),
        input_output_aliases={1: 0},
        scratch_shapes=[pltpu.SemaphoreType.DMA],
        compiler_params=params(4),
        name="weave",
    )(other, woven)


def shards(
    history,
    per_example,
    fresh,
    moment1,
    moment2,
    master,
    coef_table,
    table_index,
    step_number,
    cycle_slot,
):
    swap = [(i, i ^ 1) for i in range(16)]
    one_core = [[2 * k + c for k in range(8)] for c in range(2)]
    both = "param"
    across, near, far = ([(p, p ^ flip) for p in range(8)] for flip in (4, 1, 3))
    examples = per_example.reshape(4, 8, 2, 16, 1024)
    sums = place(squares(examples))
    sums = sums + lax.ppermute(sums, "slot", swap)
    weight, scalars = slot_weights(table_index, step_number, cycle_slot, coef_table)
    sums = sums + lax.ppermute(sums, both, far)
    sums, weight = lax.optimization_barrier((sums, weight))
    keep, send = past_parts(weight, history.reshape(16, 8, 2, 16, 1024), sums)
    got = lax.ppermute(send, "slot", swap)
    _, early = lax.optimization_barrier((send, examples))
    other = lax.ppermute(early, "slot", swap)
    sums = add(sums, lax.ppermute(sums, both, near))
    sums, keep = lax.optimization_barrier((sums, keep))
    last = lax.ppermute(sums, both, across)
    packed = pack(*clip(sums, last, examples, keep, got), other)
    parts = lax.all_to_all(packed, "slot", 0, 0, tiled=True, axis_index_groups=one_core)
    new_noise, m1, m2, master_new, weights = adam(
        scalars, parts, fresh, moment1, moment2, master
    )
    gathered = lax.all_to_all(weights, "slot", 0, 0, tiled=True, axis_index_groups=one_core)
    other_rows = lax.ppermute(gathered, "slot", swap)
    woven, *rows = store(gathered, (new_noise, m1, m2, master_new))
    return (*rows, weave(other_rows, woven).reshape(256, 1024))


def solution(mesh):
    placed = (
        P("slot", "param", None),
        P("slot", "param", None),
        P(("param", "slot"), None),
        P(("param", "slot"), None),
        P(("param", "slot"), None),
        P(("param", "slot"), None),
        P(),
        P(),
        P(),
        P(),
    )
    return jax.shard_map(
        shards,
        mesh=mesh,
        in_specs=placed,
        out_specs=(
            P(("param", "slot"), None),
            P(("param", "slot"), None),
            P(("param", "slot"), None),
            P(("param", "slot"), None),
            P("param", None),
        ),
        check_vma=False,
    )
```
